512 devices in a mesh: span: 16 (over z), seq: 32 (over y, x, core).
Axes of the slice: x: 4, y: 4, z: 16, core: 2. Of those that a mesh axis runs over, the one named last changes fastest.
Arguments:
- latents: bfloat16 [4096, 6144], P(('span', 'seq')), may hold values from -6 to 6
- levels: int32 [16], P('span'), may hold values from 0 to 15
- order: int32 [16], replicated, may hold values from 0 to 15, each once
- level_table: float32 [16, 12288], replicated, may hold values from -2 to 7, as said below
- q_gain: float32 [128], replicated, may hold values from 0.5 to 2.5
- k_gain: float32 [128], replicated, may hold values from 0.5 to 2.5
- w_qkv: bfloat16 [6144, 12288], P('span', 'seq'), may hold values from -0.078125 to 0.078125
- w_out: bfloat16 [4096, 6144], P('seq', 'span'), may hold values from -0.09375 to 0.09375
Outputs:
- mixed: bfloat16 [4096, 6144], P(('span', 'seq'))
The draws below stay inside these ranges and needn't reach their ends.
Inputs may be any that keep to these rules, and one draw needn't show every extreme that they name: Span j lies before span i when order[j] < order[i]; each span attends to itself and to the spans before it. `level_table`: the shift entries lie within -2 and 2 and every scale entry is above -1.
All inputs are finite; a program needn't handle non-finite values.
Results may differ from the reference program's by a relative error of at most 0.02.
Values may be sent and summed in bfloat16 or wider, within the bound.
A program may use at most 64 MiB of HBM per device.

```python
import math
import jax
import jax.numpy as jnp
from jax import lax

D = 6144
HEADS = 32
HD = 128
LEVELS = 16
NSPANS = 16
TOKENS = 4096
HGROUP = 1
QKVW = 12288


def draw_level_table(key, part):
    key = jax.random.fold_in(key, 7)
    gain_key, shift_key = jax.random.split(key)
    gain = jnp.exp(jax.random.uniform(gain_key, (LEVELS, D), jnp.float32, math.log(0.3), math.log(3.0)))
    shift = jnp.clip(0.5 * jax.random.normal(shift_key, (LEVELS, D), jnp.float32), -2.0, 2.0)
    return jnp.concatenate([shift, gain - 1.0], axis=1)


def set_ends(values, own_key, least, high):
    longest = values.shape.index(max(values.shape))
    spots = []
    for shift in (0, 1):
        where = [jax.random.randint(jax.random.fold_in(own_key, axis), (), 0, length) for axis, length in enumerate(values.shape)]
        where[longest] = (where[longest] + shift) % values.shape[longest]
        spots.append(tuple(where))
    return values.at[spots[0]].set(least).at[spots[1]].set(high)


def steps_of(key, shape, shards, smallest, top_value):
    loudness, own = 1.0, jax.random.fold_in(key, 6)
    for axis_at, shards_of in shards:
        steps = jnp.exp(jax.random.uniform(jax.random.fold_in(own, axis_at), (shards_of,), jnp.float32, smallest / len(shards), top_value / len(shards)))
        loudness = loudness * jnp.repeat(steps, shape[axis_at] // shards_of).reshape([-1 if axis == axis_at else 1 for axis in range(len(shape))])
    return loudness


def centred(own_key, shape, deviation, most, shards=(), kind=jnp.bfloat16):
    values = deviation * jax.random.normal(own_key, shape, jnp.float32)
    if shards:
        values = values * steps_of(own_key, shape, shards, -0.22, 0.18)
    return jnp.clip(values, -most, most).astype(kind)


def setup_inputs(seed: int = 0) -> dict:
    splits = jax.random.split(jax.random.key(seed), 9)
    latents = centred(splits[0], (TOKENS, D), 1.0, 6.0, ((0, 512),))
    levels = set_ends(jax.random.randint(splits[1], (NSPANS,), 0, LEVELS), jax.random.fold_in(splits[1], 1), 0, LEVELS - 1).astype(jnp.int32)
    order = jax.random.permutation(splits[2], NSPANS).astype(jnp.int32)
    level_table = draw_level_table(jax.random.fold_in(splits[8], 71), 0)
    q_gain = jnp.clip(jnp.exp(jax.random.uniform(splits[4], (HD,), jnp.float32, math.log(0.5), math.log(2.5))), 0.5, 2.5)
    k_gain = jnp.clip(jnp.exp(jax.random.uniform(splits[5], (HD,), jnp.float32, math.log(0.5), math.log(2.5))), 0.5, 2.5)
    w_qkv = centred(splits[6], (D, QKVW), D ** -0.5, 0.078125, ((0, 16), (1, 32)))
    w_out = centred(splits[7], (HEADS * HD, D), (HEADS * HD) ** -0.5, 0.09375, ((0, 32), (1, 16)))
    return {"latents": latents, "levels": levels, "order": order, "level_table": level_table, "q_gain": q_gain, "k_gain": k_gain, "w_qkv": w_qkv, "w_out": w_out}


def head_norm(block, gain):
    values = block.astype(jnp.float32)
    square = lax.optimization_barrier(jnp.mean(values * values, axis=-1, keepdims=True))
    return (values * lax.rsqrt(square + 1e-06) * gain).astype(jnp.bfloat16)

def reference(latents, levels, order, level_table, q_gain, k_gain, w_qkv, w_out):
    span_len = latents.shape[0] // NSPANS
    width = latents.shape[1]
    values = latents.astype(jnp.float32)
    center = values - lax.optimization_barrier(jnp.mean(values, axis=1, keepdims=True))
    spread = lax.optimization_barrier(jnp.mean(center * center, axis=1, keepdims=True))
    normed = center * lax.rsqrt(spread + 1e-06)
    table_rows = jnp.repeat(level_table[levels], span_len, axis=0)
    shift = table_rows[:, :width]
    scale = table_rows[:, width:]
    modulated = (normed * (1.0 + scale) + shift).astype(jnp.bfloat16)
    qkv = jnp.dot(modulated, w_qkv, preferred_element_type=jnp.float32).astype(jnp.bfloat16)
    qkv = qkv.reshape(qkv.shape[0], HEADS, 3, HD)
    token_order = jnp.repeat(order, span_len)
    allowed = token_order[None, :] <= token_order[:, None]

    def one_head(head):
        block = lax.dynamic_index_in_dim(qkv, head, 1, keepdims=False)
        query = head_norm(block[:, 0], q_gain)
        keys = head_norm(block[:, 1], k_gain)
        vals = block[:, 2]
        scores = jnp.dot(query, keys.T, preferred_element_type=jnp.float32) * HD ** (-0.5)
        probs = jnp.where(allowed, jnp.exp(scores), 0.0)
        row_total = lax.optimization_barrier(jnp.sum(probs, axis=1, keepdims=True))
        result = jnp.dot(probs.astype(jnp.bfloat16), vals, preferred_element_type=jnp.float32) / row_total
        return result.astype(jnp.bfloat16)
    heads_out = lax.map(one_head, jnp.arange(HEADS, dtype=jnp.int32))
    attn = jnp.transpose(heads_out, (1, 0, 2)).reshape(heads_out.shape[1], HEADS * HD)
    group_cols = HGROUP * HD

    def add_group(group, running):
        first = (group * group_cols).astype(jnp.int32)
        columns = lax.dynamic_slice_in_dim(attn, first, group_cols, 1)
        weights = lax.dynamic_slice_in_dim(w_out, first, group_cols, 0)
        term = jnp.dot(columns, weights, preferred_element_type=jnp.float32).astype(jnp.bfloat16)
        term = lax.optimization_barrier(term)
        return running + term.astype(jnp.float32)
    start_sum = jnp.zeros((attn.shape[0], w_out.shape[1]), jnp.float32)
    summed = lax.fori_loop(0, HEADS // HGROUP, add_group, start_sum)
    return summed.astype(jnp.bfloat16)
```

```python
import jax
import jax.numpy as jnp
from jax import lax
from jax.experimental import pallas as pl
from jax.experimental.pallas import tpu as pltpu
from jax.sharding import PartitionSpec as P

HD = 128
NZ = 16
BF = jnp.bfloat16
F32 = jnp.float32
MESH = pl.DeviceIdType.MESH
BLK = 384
NT = 256
HALF = 128
FAR_FIRST = (8, 7, 9, 6, 10, 5, 11, 4, 12, 3, 13, 2, 14, 1, 15)
AHEAD = 3


def dot(a, b):
    return jnp.dot(a, b, preferred_element_type=F32)


class PlaneGather:
    def __init__(self, buf, rows, x, y, at, s1, s2, rs):
        self.buf, self.rows, self.x, self.y, self.at = buf, rows, x, y, at
        self.s1, self.s2, self.rs = s1, s2, rs
        self.mine = y * 4 + x

    def part(self, block, half):
        return self.buf.at[block, pl.ds(half * self.rows, self.rows)]

    def target(self, half, phase, o):
        along_x = (half == 0) == (phase == 1)
        if along_x:
            return self.at((self.x + o) % 4, self.y)
        return self.at(self.x, (self.y + o) % 4)

    def copy(self, block, half, phase, i, slot=None):
        o = (1, 3, 2)[i]
        sem = self.s1.at[half, i] if phase == 1 else self.s2.at[half, slot, i]
        ref = self.part(block, half)
        return pltpu.make_async_remote_copy(
            src_ref=ref,
            dst_ref=ref,
            send_sem=sem,
            recv_sem=self.rs.at[half, block],
            device_id=self.target(half, phase, o),
            device_id_type=MESH,
        )

    def first(self):
        for i in range(3):
            for half in range(2):
                self.copy(self.mine, half, 1, i).start()

    def wait_block(self, block, half):
        self.copy(block, half, 1, 0).wait_recv()

    def second(self, block):
        by, bx = block // 4, block % 4
        for half in range(2):
            same = (by == self.y) if half == 0 else (bx == self.x)
            slot = bx if half == 0 else by

            @pl.when(same)
            def _(half=half, slot=slot):
                @pl.when(block != self.mine)
                def _():
                    self.wait_block(block, half)

                for i in range(3):
                    self.copy(block, half, 2, i, slot).start()

    def use(self, block):
        by, bx = block // 4, block % 4

        @pl.when(by != self.y)
        def _():
            self.wait_block(block, 0)

        @pl.when(bx != self.x)
        def _():
            self.wait_block(block, 1)

    def drain(self):
        for half in range(2):
            for i in range(3):
                self.copy(self.mine, half, 1, i).wait_send()
                for slot in range(4):
                    self.copy(self.mine, half, 2, i, slot).wait_send()


def kernel(
    lat_ref, lev_ref, ord_ref, tab_ref, qg_ref, kg_ref, w_ref, wo_ref, out_ref,
    wall, woall, xsend, xr, xin, part, cws, cwr, mask,
    qs, ks, vs, nsend, nrecv, dsend, drecv, ag, acc, sibs, sibr, osend, orecv,
    load_sem, xa_s, xa_r, sib_s, sib_r, w1, w2, wr, o1, o2, orr,
    rs_s, rs_r, qkv_s, qkv_r, nd_s, nd_r, ag_s, ag_r, oa_s, oa_r,
):
    z = lax.axis_index("span")
    s = lax.axis_index("seq")
    core = s % 2
    chip = s // 2
    x = chip % 4
    y = chip // 4

    def at(px, py):
        return (z, (py * 4 + px) * 2 + core)

    def along_z(o):
        return ((z + o) % NZ, s)

    sibling = (z, chip * 2 + 1 - core)

    load_w = pltpu.make_async_copy(w_ref, wall.at[chip], load_sem.at[0])
    load_o = pltpu.make_async_copy(wo_ref, woall.at[chip], load_sem.at[1])
    load_w.start()
    load_o.start()

    barrier = pltpu.get_barrier_semaphore()
    for o in FAR_FIRST:
        pl.semaphore_signal(barrier, inc=1, device_id=along_z(o), device_id_type=MESH)
    for o in (2, 1, 3):
        pl.semaphore_signal(barrier, inc=1, device_id=at((x + o) % 4, y), device_id_type=MESH)
        pl.semaphore_signal(barrier, inc=1, device_id=at(x, (y + o) % 4), device_id_type=MESH)
    pl.semaphore_signal(barrier, inc=1, device_id=sibling, device_id_type=MESH)

    width = lat_ref.shape[1]
    level = lev_ref[0]
    row = tab_ref[pl.ds(level, 1), :]
    values = lat_ref[...].astype(F32)
    center = values - jnp.mean(values, axis=1, keepdims=True)
    spread = jnp.mean(center * center, axis=1, keepdims=True)
    modulated = center * lax.rsqrt(spread + 1e-06) * (1.0 + row[:, width:]) + row[:, :width]
    modulated = modulated.astype(BF)
    for j in range(NZ):
        xsend[j] = modulated[:, j * BLK:(j + 1) * BLK]
    xr[core, z] = xsend[z]

    gw = PlaneGather(wall, BLK // 2, x, y, at, w1, w2, wr)
    go = PlaneGather(woall, HD // 2, x, y, at, o1, o2, orr)

    def x_copy(o):
        return pltpu.make_async_remote_copy(
            src_ref=xsend.at[(z + o) % NZ], dst_ref=xr.at[core, z],
            send_sem=xa_s.at[o], recv_sem=xa_r.at[o],
            device_id=along_z(o), device_id_type=MESH,
        )

    def x_arrival(o):
        return pltpu.make_async_remote_copy(
            src_ref=xsend.at[z], dst_ref=xr.at[core, (z + NZ - o) % NZ],
            send_sem=xa_s.at[o], recv_sem=xa_r.at[o],
            device_id=along_z(o), device_id_type=MESH,
        )

    load_w.wait()
    load_o.wait()
    pl.semaphore_wait(barrier, 22)
    for o in FAR_FIRST:
        x_copy(o).start()
    gw.first()

    key_span = (lax.broadcasted_iota(jnp.int32, (NT, HD), 0) % HALF) // 8
    query_span = (lax.broadcasted_iota(jnp.int32, (8, NT), 1) % HALF) // 8
    key_order = jnp.zeros((NT, HD), jnp.int32)
    query_order = jnp.zeros((8, NT), jnp.int32)
    for j in range(NZ):
        place = ord_ref[j]
        key_order = jnp.where(key_span == j, place, key_order)
        query_order = jnp.where(query_span == j, place, query_order)
    key_order = jnp.concatenate([key_order, key_order], axis=1)
    mask[...] = jnp.where(key_order <= query_order[0:1, :], 1.0, 0.0)

    for o in reversed(FAR_FIRST):
        x_arrival(o).wait_recv()

    def x_sib(slot):
        return pltpu.make_async_remote_copy(
            src_ref=xr.at[slot], dst_ref=xr.at[slot],
            send_sem=sib_s.at[0], recv_sem=sib_r.at[0],
            device_id=sibling, device_id_type=MESH,
        )

    x_sib(core).start()

    def place_of(t, way):
        return (z + 8 - t) % NZ if way == 0 else (z + 8 + t) % NZ

    def issue(t):
        gw.second(place_of(t, 0))
        if 0 < t < 8:
            gw.second(place_of(t, 1))

    for t in range(AHEAD):
        issue(t)

    x_sib(1 - core).wait_recv()
    xin[...] = xr[...].astype(F32).reshape(NT, BLK).astype(BF)

    def rs_copy(way, t, p):
        rows = pl.ds(p * HALF, HALF)
        return pltpu.make_async_remote_copy(
            src_ref=cws.at[way, t, rows], dst_ref=cwr.at[way, t, rows],
            send_sem=rs_s.at[way, t, p], recv_sem=rs_r.at[way, t, p],
            device_id=along_z(1 if way == 0 else NZ - 1), device_id_type=MESH,
        )

    for t in range(8):
        if t == 0:
            block = place_of(0, 0)
            gw.use(block)
            cws[0, 0, 0:HALF] = dot(xin[0:HALF], wall[block]).astype(BF)
            rs_copy(0, 0, 0).start()
            cws[1, 0, HALF:NT] = dot(xin[HALF:NT], wall[block]).astype(BF)
            rs_copy(1, 0, 1).start()
        else:
            for way in range(2):
                block = place_of(t, way)
                gw.use(block)
                part[way] = dot(xin[...], wall[block])
            for turn in range(2):
                for way in range(2):
                    p = turn if way == 0 else 1 - turn
                    rows = slice(p * HALF, (p + 1) * HALF)
                    total = part[way, rows]
                    if t > 1 or turn == 0:
                        rs_copy(way, t - 1, p).wait_recv()
                        total = total + cwr[way, t - 1, rows].astype(F32)
                    cws[way, t, rows] = total.astype(BF)
                    rs_copy(way, t, p).start()
        if t + AHEAD <= 8:
            issue(t + AHEAD)
        if t == 4:
            go.first()
        if t == 6:
            for j in range(NZ):
                go.second(jnp.int32(j))
    gw.use(z)
    part[0] = dot(xin[...], wall[z])
    for p in range(2):
        rows = slice(p * HALF, (p + 1) * HALF)
        for way in range(2):
            rs_copy(way, 7, p).wait_recv()
        total = part[0, rows] + cwr[0, 7, rows].astype(F32) + cwr[1, 7, rows].astype(F32)
        part[1, rows] = total.astype(BF).astype(F32)

    def head_norm(block, gain):
        square = jnp.mean(block * block, axis=-1, keepdims=True)
        return (block * lax.rsqrt(square + 1e-06) * gain).astype(BF)

    ks[y] = head_norm(part[1, :, HD:2 * HD], kg_ref[...])
    vs[y] = jnp.transpose(part[1, :, 2 * HD:3 * HD]).astype(BF)

    def qkv_copy(which, o, me):
        ref = (ks, vs, qs)[which].at[me]
        to = at(x, (y + o) % 4) if which < 2 else at((x + o) % 4, y)
        return pltpu.make_async_remote_copy(
            src_ref=ref, dst_ref=ref,
            send_sem=qkv_s.at[which, o], recv_sem=qkv_r.at[which, o],
            device_id=to, device_id_type=MESH,
        )

    for which in range(2):
        for o in (2, 1, 3):
            qkv_copy(which, o, y).start()
    qs[x] = head_norm(part[1, :, 0:HD], qg_ref[...])
    for o in (2, 1, 3):
        qkv_copy(2, o, x).start()
    for which in range(2):
        for o in (1, 3, 2):
            qkv_copy(which, o, (y + 4 - o) % 4).wait_recv()
    for o in (1, 3, 2):
        qkv_copy(2, o, (x + 4 - o) % 4).wait_recv()

    def nd_copy(which, o):
        src, dst = ((nsend, nrecv), (dsend, drecv))[which]
        return pltpu.make_async_remote_copy(
            src_ref=src.at[o], dst_ref=dst.at[o],
            send_sem=nd_s.at[which, o], recv_sem=nd_r.at[which, o],
            device_id=at((x + o) % 4, y), device_id_type=MESH,
        )

    def attend(queries):
        top = jnp.zeros((HD, NT), F32)
        low = jnp.zeros((1, NT), F32)
        for j in range(4):
            scores = lax.dot_general(
                ks[j], queries, (((1,), (1,)), ((), ())), preferred_element_type=F32
            ) * HD ** (-0.5)
            probs = jnp.exp(scores) * mask[...]
            low = low + jnp.sum(probs, axis=0, keepdims=True)
            top = top + dot(vs[j], probs.astype(BF))
        return top, low

    for o in (2, 1, 3):
        top, low = attend(qs[(x + o) % 4])
        nsend[o] = top.astype(BF)
        dsend[o] = jnp.broadcast_to(low, (8, NT))
        nd_copy(0, o).start()
        nd_copy(1, o).start()
    top, low = attend(qs[x])
    for o in (2, 1, 3):
        nd_copy(0, o).wait_recv()
        nd_copy(1, o).wait_recv()
        top = top + nrecv[o].astype(F32)
        low = low + drecv[o][0:1, :]
    ag[z] = jnp.transpose(top / low).astype(BF)

    def ag_copy(way, t, p, arrival=False):
        back = t + (1 if arrival else 0)
        slot = (z + NZ - back) % NZ if way == 0 else (z + back) % NZ
        ref = ag.at[slot, pl.ds(p * HALF, HALF)]
        return pltpu.make_async_remote_copy(
            src_ref=ref, dst_ref=ref,
            send_sem=ag_s.at[way, t, p], recv_sem=ag_r.at[way, t, p],
            device_id=along_z(1 if way == 0 else NZ - 1), device_id_type=MESH,
        )

    for p in range(2):
        for way in range(2):
            ag_copy(way, 0, p).start()
    for j in range(NZ):
        go.use(jnp.int32(j))
    acc[...] = dot(ag[z], woall[z])
    for t in range(1, 8):
        for turn in range(2):
            for way in range(2):
                p = turn if way == 0 else 1 - turn
                ag_copy(way, t - 1, p, True).wait_recv()
                if t < 7 or turn == 0:
                    ag_copy(way, t, p).start()
        a, b = (z + NZ - t) % NZ, (z + t) % NZ
        acc[...] += dot(ag[a], woall[a]) + dot(ag[b], woall[b])
    ag_copy(0, 7, 0, True).wait_recv()
    ag_copy(1, 7, 1, True).wait_recv()
    a = (z + 8) % NZ
    acc[...] += dot(ag[a], woall[a])

    sibs[...] = acc[pl.ds(pl.multiple_of((1 - core) * HALF, HALF), HALF)].astype(BF)

    sib = pltpu.make_async_remote_copy(
        src_ref=sibs, dst_ref=sibr, send_sem=sib_s.at[1], recv_sem=sib_r.at[1],
        device_id=sibling, device_id_type=MESH,
    )
    sib.start()
    own = acc[pl.ds(pl.multiple_of(core * HALF, HALF), HALF)]
    sib.wait_recv()
    osend[...] = (own + sibr[...].astype(F32)).reshape(NZ, 8, BLK).astype(BF)

    def out_copy(o, arrival=False):
        slot = (z + NZ - o) % NZ if arrival else z
        return pltpu.make_async_remote_copy(
            src_ref=osend.at[(z + o) % NZ], dst_ref=orecv.at[slot],
            send_sem=oa_s.at[o], recv_sem=oa_r.at[o],
            device_id=along_z(o), device_id_type=MESH,
        )

    for o in FAR_FIRST:
        out_copy(o).start()
    orecv[z] = osend[z]

    for o in range(1, NZ):
        x_copy(o).wait_send()
    x_sib(core).wait_send()
    gw.drain()
    go.drain()
    for way in range(2):
        for t in range(8):
            for p in range(2):
                if t > 0 or p == way:
                    rs_copy(way, t, p).wait_send()
                if t < 7 or p == way:
                    ag_copy(way, t, p).wait_send()
    for o in (1, 2, 3):
        for which in range(3):
            qkv_copy(which, o, y if which < 2 else x).wait_send()
        for which in range(2):
            nd_copy(which, o).wait_send()
    sib.wait_send()

    for o in reversed(FAR_FIRST):
        out_copy(o, True).wait_recv()
    for o in range(1, NZ):
        out_copy(o).wait_send()
    for j in range(NZ):
        out_ref[:, j * BLK:(j + 1) * BLK] = orecv[j]


def body(latents, levels, order, level_table, q_gain, k_gain, w_qkv, w_out):
    vmem = pl.BlockSpec(memory_space=pltpu.VMEM)
    smem = pl.BlockSpec(memory_space=pltpu.SMEM)
    hbm = pl.BlockSpec(memory_space=pl.ANY)
    dma = pltpu.SemaphoreType.DMA
    return pl.pallas_call(
        kernel,
        out_shape=jax.ShapeDtypeStruct(latents.shape, BF),
        in_specs=[vmem, smem, smem, vmem, vmem, vmem, hbm, hbm],
        out_specs=vmem,
        scratch_shapes=[
            pltpu.VMEM((16, BLK, BLK), BF),
            pltpu.VMEM((16, HD, BLK), BF),
            pltpu.VMEM((NZ, 8, BLK), BF),
            pltpu.VMEM((2, NZ, 8, BLK), BF),
            pltpu.VMEM((NT, BLK), BF),
            pltpu.VMEM((2, NT, BLK), F32),
            pltpu.VMEM((2, 8, NT, BLK), BF),
            pltpu.VMEM((2, 8, NT, BLK), BF),
            pltpu.VMEM((NT, NT), F32),
            pltpu.VMEM((4, NT, HD), BF),
            pltpu.VMEM((4, NT, HD), BF),
            pltpu.VMEM((4, HD, NT), BF),
            pltpu.VMEM((4, HD, NT), BF),
            pltpu.VMEM((4, HD, NT), BF),
            pltpu.VMEM((4, 8, NT), F32),
            pltpu.VMEM((4, 8, NT), F32),
            pltpu.VMEM((NZ, NT, HD), BF),
            pltpu.VMEM((NT, BLK), F32),
            pltpu.VMEM((HALF, BLK), BF),
            pltpu.VMEM((HALF, BLK), BF),
            pltpu.VMEM((NZ, 8, BLK), BF),
            pltpu.VMEM((NZ, 8, BLK), BF),
            dma((2,)),
            dma((NZ,)), dma((NZ,)),
            dma((2,)), dma((2,)),
            dma((2, 3)), dma((2, 4, 3)), dma((2, 16)),
            dma((2, 3)), dma((2, 4, 3)), dma((2, 16)),
            dma((2, 8, 2)), dma((2, 8, 2)),
            dma((3, 4)), dma((3, 4)),
            dma((2, 4)), dma((2, 4)),
            dma((2, 8, 2)), dma((2, 8, 2)),
            dma((NZ,)), dma((NZ,)),
        ],
        compiler_params=pltpu.CompilerParams(
            collective_id=0, has_side_effects=True, vmem_limit_bytes=40 * 2**20
        ),
        name="spans",
    )(
        latents, levels, order, level_table,
        q_gain.reshape(1, HD), k_gain.reshape(1, HD), w_qkv, w_out,
    )


def solution(mesh):
    placed = (
        P(("span", "seq"), None),
        P("span"),
        P(),
        P(),
        P(),
        P(),
        P("span", "seq"),
        P("seq", "span"),
    )
    return jax.shard_map(
        body, mesh=mesh, in_specs=placed, out_specs=P(("span", "seq"), None), check_vma=False
    )
```

```python
import jax
import jax.numpy as jnp
from jax import lax
from jax.experimental import pallas as pl
from jax.experimental.pallas import tpu as pltpu
from jax.sharding import PartitionSpec as P

HD = 128
NZ = 16
BF = jnp.bfloat16
F32 = jnp.float32
MESH = pl.DeviceIdType.MESH
BLK = 384
NT = 256
HALF = 128
FAR_FIRST = (8, 7, 9, 6, 10, 5, 11, 4, 12, 3, 13, 2, 14, 1, 15)
FIRST = 4


def dot(a, b):
    return jnp.dot(a, b, preferred_element_type=F32)


class PlaneGather:
    def __init__(self, buf, rows, x, y, at, s1, s2, rs):
        self.buf, self.rows, self.x, self.y, self.at = buf, rows, x, y, at
        self.s1, self.s2, self.rs = s1, s2, rs
        self.mine = ((x + 4 - y) % 4) * 4 + y

    @staticmethod
    def place(block):
        return block % 4, (block + block // 4) % 4

    def part(self, block, half):
        return self.buf.at[block, pl.ds(half * self.rows, self.rows)]

    def target(self, half, phase, o):
        along_x = (half == 0) == (phase == 1)
        if along_x:
            return self.at((self.x + o) % 4, self.y)
        return self.at(self.x, (self.y + o) % 4)

    def copy(self, block, half, phase, i, slot=None):
        o = (1, 3, 2)[i]
        sem = self.s1.at[half, i] if phase == 1 else self.s2.at[half, slot, i]
        ref = self.part(block, half)
        return pltpu.make_async_remote_copy(
            src_ref=ref,
            dst_ref=ref,
            send_sem=sem,
            recv_sem=self.rs.at[half, block],
            device_id=self.target(half, phase, o),
            device_id_type=MESH,
        )

    def first(self):
        for i in range(3):
            for half in range(2):
                self.copy(self.mine, half, 1, i).start()

    def wait_block(self, block, half):
        self.copy(block, half, 1, 0).wait_recv()

    def second(self, block):
        by, bx = self.place(block)
        for half in range(2):
            same = (by == self.y) if half == 0 else (bx == self.x)
            slot = bx if half == 0 else by

            @pl.when(same)
            def _(half=half, slot=slot):
                @pl.when(block != self.mine)
                def _():
                    self.wait_block(block, half)

                for i in range(3):
                    self.copy(block, half, 2, i, slot).start()

    def use(self, block):
        by, bx = self.place(block)

        @pl.when(by != self.y)
        def _():
            self.wait_block(block, 0)

        @pl.when(bx != self.x)
        def _():
            self.wait_block(block, 1)

    def drain(self):
        for half in range(2):
            for i in range(3):
                self.copy(self.mine, half, 1, i).wait_send()
                for slot in range(4):
                    self.copy(self.mine, half, 2, i, slot).wait_send()


def kernel(
    lat_hbm, lev_ref, ord_ref, tab_hbm, qg_hbm, kg_hbm, w_ref, wo_ref, out_ref,
    lat_ref, tab_ref, qg_ref, kg_ref, wall, woall, xsend, xr, xin, part, cws, cwr, mask,
    qs, ks, vs, nsend, nrecv, dsend, drecv, ag, acc, sibs, sibr, osend, orecv,
    load_sem, xa_s, xa_r, sib_s, sib_r, w1, w2, wr, o1, o2, orr,
    rs_s, rs_r, qkv_s, qkv_r, nd_s, nd_r, ag_s, ag_r, oa_s, oa_r,
):
    z = lax.axis_index("span")
    s = lax.axis_index("seq")
    core = s % 2
    chip = s // 2
    x = chip % 4
    y = chip // 4

    def at(px, py):
        return (z, (py * 4 + px) * 2 + core)

    def along_z(o):
        return ((z + o) % NZ, s)

    sibling = (z, chip * 2 + 1 - core)

    gw = PlaneGather(wall, BLK // 2, x, y, at, w1, w2, wr)
    go = PlaneGather(woall, HD // 2, x, y, at, o1, o2, orr)
    loads = [
        pltpu.make_async_copy(src, dst, load_sem.at[i])
        for i, (src, dst) in enumerate((
            (lat_hbm, lat_ref), (tab_hbm, tab_ref), (w_ref, wall.at[gw.mine]),
            (wo_ref, woall.at[go.mine]), (qg_hbm, qg_ref), (kg_hbm, kg_ref),
        ))
    ]
    for load in loads:
        load.start()

    barrier = pltpu.get_barrier_semaphore()
    for o in FAR_FIRST:
        pl.semaphore_signal(barrier, inc=1, device_id=along_z(o), device_id_type=MESH)
    for o in (2, 1, 3):
        pl.semaphore_signal(barrier, inc=1, device_id=at((x + o) % 4, y), device_id_type=MESH)
        pl.semaphore_signal(barrier, inc=1, device_id=at(x, (y + o) % 4), device_id_type=MESH)
    pl.semaphore_signal(barrier, inc=1, device_id=sibling, device_id_type=MESH)

    for load in loads:
        load.wait()
    width = lat_ref.shape[1]
    level = lev_ref[0]
    row = tab_ref[pl.ds(level, 1), :]
    values = lat_ref[...].astype(F32)
    center = values - jnp.mean(values, axis=1, keepdims=True)
    spread = jnp.mean(center * center, axis=1, keepdims=True)
    modulated = center * lax.rsqrt(spread + 1e-06) * (1.0 + row[:, width:]) + row[:, :width]
    modulated = modulated.astype(BF)
    for j in range(NZ):
        xsend[j] = modulated[:, j * BLK:(j + 1) * BLK]
    xr[core, z] = xsend[z]

    def x_copy(o):
        return pltpu.make_async_remote_copy(
            src_ref=xsend.at[(z + o) % NZ], dst_ref=xr.at[core, z],
            send_sem=xa_s.at[o], recv_sem=xa_r.at[o],
            device_id=along_z(o), device_id_type=MESH,
        )

    def x_arrival(o):
        return pltpu.make_async_remote_copy(
            src_ref=xsend.at[z], dst_ref=xr.at[core, (z + NZ - o) % NZ],
            send_sem=xa_s.at[o], recv_sem=xa_r.at[o],
            device_id=along_z(o), device_id_type=MESH,
        )

    pl.semaphore_wait(barrier, 22)
    for o in FAR_FIRST:
        x_copy(o).start()
    gw.first()

    key_span = (lax.broadcasted_iota(jnp.int32, (NT, HD), 0) % HALF) // 8
    query_span = (lax.broadcasted_iota(jnp.int32, (8, NT), 1) % HALF) // 8
    key_order = jnp.zeros((NT, HD), jnp.int32)
    query_order = jnp.zeros((8, NT), jnp.int32)
    for j in range(NZ):
        place = ord_ref[j]
        key_order = jnp.where(key_span == j, place, key_order)
        query_order = jnp.where(query_span == j, place, query_order)
    key_order = jnp.concatenate([key_order, key_order], axis=1)
    mask[...] = jnp.where(key_order <= query_order[0:1, :], 1.0, 0.0)

    for o in reversed(FAR_FIRST):
        x_arrival(o).wait_recv()

    def x_sib(slot):
        return pltpu.make_async_remote_copy(
            src_ref=xr.at[slot], dst_ref=xr.at[slot],
            send_sem=sib_s.at[0], recv_sem=sib_r.at[0],
            device_id=sibling, device_id_type=MESH,
        )

    x_sib(core).start()

    def place_of(t, way):
        return (z + 8 - t) % NZ if way == 0 else (z + 8 + t) % NZ

    order_of_use = [place_of(0, 0)]
    for t in range(1, 8):
        order_of_use += [place_of(t, 0), place_of(t, 1)]
    order_of_use.append(z)
    for block in order_of_use[:FIRST]:
        gw.second(block)

    x_sib(1 - core).wait_recv()
    xin[...] = xr[...].astype(F32).reshape(NT, BLK).astype(BF)

    def rs_copy(way, t, p):
        rows = pl.ds(p * HALF, HALF)
        return pltpu.make_async_remote_copy(
            src_ref=cws.at[way, t, rows], dst_ref=cwr.at[way, t, rows],
            send_sem=rs_s.at[way, t, p], recv_sem=rs_r.at[way, t, p],
            device_id=along_z(1 if way == 0 else NZ - 1), device_id_type=MESH,
        )

    for t in range(8):
        if t == 0:
            block = place_of(0, 0)
            gw.use(block)
            cws[0, 0, 0:HALF] = dot(xin[0:HALF], wall[block]).astype(BF)
            rs_copy(0, 0, 0).start()
            cws[1, 0, HALF:NT] = dot(xin[HALF:NT], wall[block]).astype(BF)
            rs_copy(1, 0, 1).start()
        else:
            for way in range(2):
                block = place_of(t, way)
                gw.use(block)
                part[way] = dot(xin[...], wall[block])
            for turn in range(2):
                for way in range(2):
                    p = turn if way == 0 else 1 - turn
                    rows = slice(p * HALF, (p + 1) * HALF)
                    total = part[way, rows]
                    if t > 1 or turn == 0:
                        rs_copy(way, t - 1, p).wait_recv()
                        total = total + cwr[way, t - 1, rows].astype(F32)
                    cws[way, t, rows] = total.astype(BF)
                    rs_copy(way, t, p).start()
        for block in order_of_use[FIRST + 2 * t:FIRST + 2 * t + 2]:
            gw.second(block)
        if t == 3:
            go.first()
        if t > 3:
            for j in range(4 * (t - 4), 4 * (t - 3)):
                go.second(jnp.int32(j))
    gw.use(z)
    part[0] = dot(xin[...], wall[z])
    for p in range(2):
        rows = slice(p * HALF, (p + 1) * HALF)
        for way in range(2):
            rs_copy(way, 7, p).wait_recv()
        total = part[0, rows] + cwr[0, 7, rows].astype(F32) + cwr[1, 7, rows].astype(F32)
        part[1, rows] = total.astype(BF).astype(F32)

    def head_norm(block, gain):
        square = jnp.mean(block * block, axis=-1, keepdims=True)
        return (block * lax.rsqrt(square + 1e-06) * gain).astype(BF)

    ks[y] = head_norm(part[1, :, HD:2 * HD], kg_ref[...])
    vs[y] = jnp.transpose(part[1, :, 2 * HD:3 * HD]).astype(BF)

    def qkv_copy(which, o, me):
        ref = (ks, vs, qs)[which].at[me]
        to = at(x, (y + o) % 4) if which < 2 else at((x + o) % 4, y)
        return pltpu.make_async_remote_copy(
            src_ref=ref, dst_ref=ref,
            send_sem=qkv_s.at[which, o], recv_sem=qkv_r.at[which, o],
            device_id=to, device_id_type=MESH,
        )

    for which in range(2):
        for o in (2, 1, 3):
            qkv_copy(which, o, y).start()
    qs[x] = head_norm(part[1, :, 0:HD], qg_ref[...])
    for o in (2, 1, 3):
        qkv_copy(2, o, x).start()
    for which in range(2):
        for o in (1, 3, 2):
            qkv_copy(which, o, (y + 4 - o) % 4).wait_recv()
    for o in (1, 3, 2):
        qkv_copy(2, o, (x + 4 - o) % 4).wait_recv()

    def nd_copy(which, o):
        src, dst = ((nsend, nrecv), (dsend, drecv))[which]
        return pltpu.make_async_remote_copy(
            src_ref=src.at[o], dst_ref=dst.at[o],
            send_sem=nd_s.at[which, o], recv_sem=nd_r.at[which, o],
            device_id=at((x + o) % 4, y), device_id_type=MESH,
        )

    def attend(queries):
        top = jnp.zeros((HD, NT), F32)
        low = jnp.zeros((1, NT), F32)
        for j in range(4):
            scores = lax.dot_general(
                ks[j], queries, (((1,), (1,)), ((), ())), preferred_element_type=F32
            ) * HD ** (-0.5)
            probs = jnp.exp(scores) * mask[...]
            low = low + jnp.sum(probs, axis=0, keepdims=True)
            top = top + dot(vs[j], probs.astype(BF))
        return top, low

    for o in (2, 1, 3):
        top, low = attend(qs[(x + o) % 4])
        nsend[o] = top.astype(BF)
        dsend[o] = jnp.broadcast_to(low, (8, NT))
        nd_copy(0, o).start()
        nd_copy(1, o).start()
    top, low = attend(qs[x])
    for o in (2, 1, 3):
        nd_copy(0, o).wait_recv()
        nd_copy(1, o).wait_recv()
        top = top + nrecv[o].astype(F32)
        low = low + drecv[o][0:1, :]
    ag[z] = jnp.transpose(top / low).astype(BF)

    def ag_copy(way, t, p, arrival=False):
        back = t + (1 if arrival else 0)
        slot = (z + NZ - back) % NZ if way == 0 else (z + back) % NZ
        ref = ag.at[slot, pl.ds(p * HALF, HALF)]
        return pltpu.make_async_remote_copy(
            src_ref=ref, dst_ref=ref,
            send_sem=ag_s.at[way, t, p], recv_sem=ag_r.at[way, t, p],
            device_id=along_z(1 if way == 0 else NZ - 1), device_id_type=MESH,
        )

    for p in range(2):
        for way in range(2):
            ag_copy(way, 0, p).start()
    for j in range(NZ):
        go.use(jnp.int32(j))
    for t in range(1, 8):
        for turn in range(2):
            for way in range(2):
                p = turn if way == 0 else 1 - turn
                ag_copy(way, t - 1, p, True).wait_recv()
                if t < 7 or turn == 0:
                    ag_copy(way, t, p).start()
    ag_copy(0, 7, 0, True).wait_recv()
    ag_copy(1, 7, 1, True).wait_recv()
    gathered = jnp.concatenate([ag[j] for j in range(NZ)], axis=1)
    acc[...] = dot(gathered, woall[...].reshape(NZ * HD, BLK))

    sibs[...] = acc[pl.ds(pl.multiple_of((1 - core) * HALF, HALF), HALF)].astype(BF)

    sib = pltpu.make_async_remote_copy(
        src_ref=sibs, dst_ref=sibr, send_sem=sib_s.at[1], recv_sem=sib_r.at[1],
        device_id=sibling, device_id_type=MESH,
    )
    sib.start()
    own = acc[pl.ds(pl.multiple_of(core * HALF, HALF), HALF)]
    sib.wait_recv()
    osend[...] = (own + sibr[...].astype(F32)).reshape(NZ, 8, BLK).astype(BF)

    def out_copy(o, arrival=False):
        slot = (z + NZ - o) % NZ if arrival else z
        return pltpu.make_async_remote_copy(
            src_ref=osend.at[(z + o) % NZ], dst_ref=orecv.at[slot],
            send_sem=oa_s.at[o], recv_sem=oa_r.at[o],
            device_id=along_z(o), device_id_type=MESH,
        )

    for o in FAR_FIRST:
        out_copy(o).start()
    orecv[z] = osend[z]

    for o in range(1, NZ):
        x_copy(o).wait_send()
    x_sib(core).wait_send()
    gw.drain()
    go.drain()
    for way in range(2):
        for t in range(8):
            for p in range(2):
                if t > 0 or p == way:
                    rs_copy(way, t, p).wait_send()
                if t < 7 or p == way:
                    ag_copy(way, t, p).wait_send()
    for o in (1, 2, 3):
        for which in range(3):
            qkv_copy(which, o, y if which < 2 else x).wait_send()
        for which in range(2):
            nd_copy(which, o).wait_send()
    sib.wait_send()

    for o in reversed(FAR_FIRST):
        out_copy(o, True).wait_recv()
    for o in range(1, NZ):
        out_copy(o).wait_send()
    for j in range(NZ):
        out_ref[:, j * BLK:(j + 1) * BLK] = orecv[j]


def body(latents, levels, order, level_table, q_gain, k_gain, w_qkv, w_out):
    vmem = pl.BlockSpec(memory_space=pltpu.VMEM)
    smem = pl.BlockSpec(memory_space=pltpu.SMEM)
    hbm = pl.BlockSpec(memory_space=pl.ANY)
    dma = pltpu.SemaphoreType.DMA
    return pl.pallas_call(
        kernel,
        out_shape=jax.ShapeDtypeStruct(latents.shape, BF),
        in_specs=[hbm, smem, smem, hbm, hbm, hbm, hbm, hbm],
        out_specs=vmem,
        scratch_shapes=[
            pltpu.VMEM(latents.shape, BF),
            pltpu.VMEM(level_table.shape, F32),
            pltpu.VMEM((1, HD), F32),
            pltpu.VMEM((1, HD), F32),
            pltpu.VMEM((16, BLK, BLK), BF),
            pltpu.VMEM((16, HD, BLK), BF),
            pltpu.VMEM((NZ, 8, BLK), BF),
            pltpu.VMEM((2, NZ, 8, BLK), BF),
            pltpu.VMEM((NT, BLK), BF),
            pltpu.VMEM((2, NT, BLK), F32),
            pltpu.VMEM((2, 8, NT, BLK), BF),
            pltpu.VMEM((2, 8, NT, BLK), BF),
            pltpu.VMEM((NT, NT), F32),
            pltpu.VMEM((4, NT, HD), BF),
            pltpu.VMEM((4, NT, HD), BF),
            pltpu.VMEM((4, HD, NT), BF),
            pltpu.VMEM((4, HD, NT), BF),
            pltpu.VMEM((4, HD, NT), BF),
            pltpu.VMEM((4, 8, NT), F32),
            pltpu.VMEM((4, 8, NT), F32),
            pltpu.VMEM((NZ, NT, HD), BF),
            pltpu.VMEM((NT, BLK), F32),
            pltpu.VMEM((HALF, BLK), BF),
            pltpu.VMEM((HALF, BLK), BF),
            pltpu.VMEM((NZ, 8, BLK), BF),
            pltpu.VMEM((NZ, 8, BLK), BF),
            dma((6,)),
            dma((NZ,)), dma((NZ,)),
            dma((2,)), dma((2,)),
            dma((2, 3)), dma((2, 4, 3)), dma((2, 16)),
            dma((2, 3)), dma((2, 4, 3)), dma((2, 16)),
            dma((2, 8, 2)), dma((2, 8, 2)),
            dma((3, 4)), dma((3, 4)),
            dma((2, 4)), dma((2, 4)),
            dma((2, 8, 2)), dma((2, 8, 2)),
            dma((NZ,)), dma((NZ,)),
        ],
        compiler_params=pltpu.CompilerParams(
            collective_id=0, has_side_effects=True, vmem_limit_bytes=60 * 2**20
        ),
        name="spans",
    )(
        latents, levels, order, level_table,
        q_gain.reshape(1, HD), k_gain.reshape(1, HD), w_qkv, w_out,
    )


def solution(mesh):
    placed = (
        P(("span", "seq"), None),
        P("span"),
        P(),
        P(),
        P(),
        P(),
        P("span", "seq"),
        P("seq", "span"),
    )
    return jax.shard_map(
        body, mesh=mesh, in_specs=placed, out_specs=P(("span", "seq"), None), check_vma=False
    )
```

```python
import jax
import jax.numpy as jnp
from jax import lax
from jax.experimental import pallas as pl
from jax.experimental.pallas import tpu as pltpu
from jax.sharding import PartitionSpec as P

HD = 128
NZ = 16
BF = jnp.bfloat16
F32 = jnp.float32
MESH = pl.DeviceIdType.MESH
BLK = 384
NT = 256
HALF = 128
FAR_FIRST = (8, 7, 9, 6, 10, 5, 11, 4, 12, 3, 13, 2, 14, 1, 15)
FIRST = 4
WO_AT = {0: 3, 3: 4, 6: 5}
PIECES = 2
WIDE = 8 * BLK // PIECES


def dot(a, b):
    return jnp.dot(a, b, preferred_element_type=F32)


class PlaneGather:
    def __init__(self, buf, rows, x, y, at, s1, s2, rs):
        self.buf, self.rows, self.x, self.y, self.at = buf, rows, x, y, at
        self.s1, self.s2, self.rs = s1, s2, rs
        self.mine = ((x + 4 - y) % 4) * 4 + y

    @staticmethod
    def place(block):
        return block % 4, (block + block // 4) % 4

    def part(self, block, half):
        return self.buf.at[block, pl.ds(half * self.rows, self.rows)]

    def target(self, half, phase, o):
        along_x = (half == 0) == (phase == 1)
        if along_x:
            return self.at((self.x + o) % 4, self.y)
        return self.at(self.x, (self.y + o) % 4)

    def copy(self, block, half, phase, i, slot=None):
        o = (1, 3, 2)[i]
        sem = self.s1.at[half, i] if phase == 1 else self.s2.at[half, slot, i]
        ref = self.part(block, half)
        return pltpu.make_async_remote_copy(
            src_ref=ref,
            dst_ref=ref,
            send_sem=sem,
            recv_sem=self.rs.at[half, block],
            device_id=self.target(half, phase, o),
            device_id_type=MESH,
        )

    def first(self):
        for i in range(3):
            for half in range(2):
                self.copy(self.mine, half, 1, i).start()

    def wait_block(self, block, half):
        self.copy(block, half, 1, 0).wait_recv()

    def second(self, block):
        by, bx = self.place(block)
        for half in range(2):
            same = (by == self.y) if half == 0 else (bx == self.x)
            slot = bx if half == 0 else by

            @pl.when(same)
            def _(half=half, slot=slot):
                @pl.when(block != self.mine)
                def _():
                    self.wait_block(block, half)

                for i in range(3):
                    self.copy(block, half, 2, i, slot).start()

    def use(self, block):
        by, bx = self.place(block)

        @pl.when(by != self.y)
        def _():
            self.wait_block(block, 0)

        @pl.when(bx != self.x)
        def _():
            self.wait_block(block, 1)

    def drain(self):
        for half in range(2):
            for i in range(3):
                self.copy(self.mine, half, 1, i).wait_send()
                for slot in range(4):
                    self.copy(self.mine, half, 2, i, slot).wait_send()


def kernel(
    lat_hbm, lev_ref, ord_ref, tab_hbm, qg_hbm, kg_hbm, w_ref, wo_ref, out_ref,
    lat_ref, tab_ref, qg_ref, kg_ref, wall, xsend, xr, xin, part, cws, cwr, mask,
    qs, ks, vs, nsend, nrecv, dsend, drecv, wog, asend, brecv, ts, tr, us, ur,
    load_sem, xa_s, xa_r, sib_s, sib_r, w1, w2, wr, wo_s, wo_r, ws_s, ws_r,
    rs_s, rs_r, qkv_s, qkv_r, nd_s, nd_r, aa_s, aa_r, t_s, t_r, u_s, u_r,
):
    z = lax.axis_index("span")
    s = lax.axis_index("seq")
    core = s % 2
    chip = s // 2
    x = chip % 4
    y = chip // 4

    def at(px, py):
        return (z, (py * 4 + px) * 2 + core)

    def along_z(o):
        return ((z + o) % NZ, s)

    sibling = (z, chip * 2 + 1 - core)

    gw = PlaneGather(wall, BLK // 2, x, y, at, w1, w2, wr)
    loads = [
        pltpu.make_async_copy(src, dst, load_sem.at[i])
        for i, (src, dst) in enumerate((
            (lat_hbm, lat_ref), (tab_hbm, tab_ref), (w_ref, wall.at[gw.mine]),
            (wo_ref, wog.at[core, z]), (qg_hbm, qg_ref), (kg_hbm, kg_ref),
        ))
    ]
    for load in loads:
        load.start()

    barrier = pltpu.get_barrier_semaphore()
    for o in FAR_FIRST:
        pl.semaphore_signal(barrier, inc=1, device_id=along_z(o), device_id_type=MESH)
    for o in (2, 1, 3):
        pl.semaphore_signal(barrier, inc=1, device_id=at((x + o) % 4, y), device_id_type=MESH)
        pl.semaphore_signal(barrier, inc=1, device_id=at(x, (y + o) % 4), device_id_type=MESH)
    pl.semaphore_signal(barrier, inc=1, device_id=sibling, device_id_type=MESH)

    for load in loads:
        load.wait()
    width = lat_ref.shape[1]
    level = lev_ref[0]
    row = tab_ref[pl.ds(level, 1), :]
    values = lat_ref[...].astype(F32)
    center = values - jnp.mean(values, axis=1, keepdims=True)
    spread = jnp.mean(center * center, axis=1, keepdims=True)
    modulated = center * lax.rsqrt(spread + 1e-06) * (1.0 + row[:, width:]) + row[:, :width]
    modulated = modulated.astype(BF)
    for j in range(NZ):
        xsend[j] = modulated[:, j * BLK:(j + 1) * BLK]
    xr[core, z] = xsend[z]

    def x_copy(o):
        return pltpu.make_async_remote_copy(
            src_ref=xsend.at[(z + o) % NZ], dst_ref=xr.at[core, z],
            send_sem=xa_s.at[o], recv_sem=xa_r.at[o],
            device_id=along_z(o), device_id_type=MESH,
        )

    def x_arrival(o):
        return pltpu.make_async_remote_copy(
            src_ref=xsend.at[z], dst_ref=xr.at[core, (z + NZ - o) % NZ],
            send_sem=xa_s.at[o], recv_sem=xa_r.at[o],
            device_id=along_z(o), device_id_type=MESH,
        )

    pl.semaphore_wait(barrier, 22)
    gw.first()
    for o in FAR_FIRST:
        x_copy(o).start()

    def wo_copy(way, t, arrival=False):
        back = t + (1 if arrival else 0)
        slot = (z + NZ - back) % NZ if way == 0 else (z + back) % NZ
        ref = wog.at[core, slot]
        if t == 7:
            ref = wog.at[core, slot, pl.ds(way * (HD // 2), HD // 2)]
        return pltpu.make_async_remote_copy(
            src_ref=ref, dst_ref=ref,
            send_sem=wo_s.at[way, t], recv_sem=wo_r.at[way, t],
            device_id=along_z(1 if way == 0 else NZ - 1), device_id_type=MESH,
        )

    def wo_sib(side, o):
        ref = wog.at[side, (z + o) % NZ]
        return pltpu.make_async_remote_copy(
            src_ref=ref, dst_ref=ref, send_sem=ws_s.at[o], recv_sem=ws_r.at[o],
            device_id=sibling, device_id_type=MESH,
        )

    def wo_step(t):
        if t > 0:
            for way in range(2):
                wo_copy(way, t - 1, True).wait_recv()
        if t < 8:
            for way in range(2):
                wo_copy(way, t).start()
        if t == 0 or t == 8:
            wo_sib(core, t).start()
        else:
            wo_sib(core, t).start()
            wo_sib(core, NZ - t).start()

    wo_step(0)

    key_span = (lax.broadcasted_iota(jnp.int32, (NT, HD), 0) % HALF) // 8
    query_span = (lax.broadcasted_iota(jnp.int32, (8, NT), 1) % HALF) // 8
    key_order = jnp.zeros((NT, HD), jnp.int32)
    query_order = jnp.zeros((8, NT), jnp.int32)
    for j in range(NZ):
        place = ord_ref[j]
        key_order = jnp.where(key_span == j, place, key_order)
        query_order = jnp.where(query_span == j, place, query_order)
    key_order = jnp.concatenate([key_order, key_order], axis=1)
    mask[...] = jnp.where(key_order <= query_order[0:1, :], 1.0, 0.0)

    for o in reversed(FAR_FIRST):
        x_arrival(o).wait_recv()

    def x_sib(slot):
        return pltpu.make_async_remote_copy(
            src_ref=xr.at[slot], dst_ref=xr.at[slot],
            send_sem=sib_s.at[0], recv_sem=sib_r.at[0],
            device_id=sibling, device_id_type=MESH,
        )

    x_sib(core).start()

    def place_of(t, way):
        return (z + 8 - t) % NZ if way == 0 else (z + 8 + t) % NZ

    order_of_use = [place_of(0, 0)]
    for t in range(1, 8):
        order_of_use += [place_of(t, 0), place_of(t, 1)]
    order_of_use.append(z)
    for block in order_of_use[:FIRST]:
        gw.second(block)

    wo_step(1)
    x_sib(1 - core).wait_recv()
    xin[...] = xr[...].astype(F32).reshape(NT, BLK).astype(BF)

    wo_step(2)

    def rs_copy(way, t, p):
        rows = pl.ds(p * HALF, HALF)
        return pltpu.make_async_remote_copy(
            src_ref=cws.at[way, t, rows], dst_ref=cwr.at[way, t, rows],
            send_sem=rs_s.at[way, t, p], recv_sem=rs_r.at[way, t, p],
            device_id=along_z(1 if way == 0 else NZ - 1), device_id_type=MESH,
        )

    for t in range(8):
        if t == 0:
            block = place_of(0, 0)
            gw.use(block)
            cws[0, 0, 0:HALF] = dot(xin[0:HALF], wall[block]).astype(BF)
            rs_copy(0, 0, 0).start()
            cws[1, 0, HALF:NT] = dot(xin[HALF:NT], wall[block]).astype(BF)
            rs_copy(1, 0, 1).start()
        else:
            for way in range(2):
                block = place_of(t, way)
                gw.use(block)
                part[way] = dot(xin[...], wall[block])
            for turn in range(2):
                for way in range(2):
                    p = turn if way == 0 else 1 - turn
                    rows = slice(p * HALF, (p + 1) * HALF)
                    total = part[way, rows]
                    if t > 1 or turn == 0:
                        rs_copy(way, t - 1, p).wait_recv()
                        total = total + cwr[way, t - 1, rows].astype(F32)
                    cws[way, t, rows] = total.astype(BF)
                    rs_copy(way, t, p).start()
        for block in order_of_use[FIRST + 2 * t:FIRST + 2 * t + 2]:
            gw.second(block)
        if t in WO_AT:
            wo_step(WO_AT[t])
    gw.use(z)
    part[0] = dot(xin[...], wall[z])
    for p in range(2):
        rows = slice(p * HALF, (p + 1) * HALF)
        for way in range(2):
            rs_copy(way, 7, p).wait_recv()
        total = part[0, rows] + cwr[0, 7, rows].astype(F32) + cwr[1, 7, rows].astype(F32)
        part[1, rows] = total.astype(BF).astype(F32)

    def head_norm(block, gain):
        square = jnp.mean(block * block, axis=-1, keepdims=True)
        return (block * lax.rsqrt(square + 1e-06) * gain).astype(BF)

    ks[y] = head_norm(part[1, :, HD:2 * HD], kg_ref[...])
    vs[y] = jnp.transpose(part[1, :, 2 * HD:3 * HD]).astype(BF)

    def qkv_copy(which, o, me):
        ref = (ks, vs, qs)[which].at[me]
        to = at(x, (y + o) % 4) if which < 2 else at((x + o) % 4, y)
        return pltpu.make_async_remote_copy(
            src_ref=ref, dst_ref=ref,
            send_sem=qkv_s.at[which, o], recv_sem=qkv_r.at[which, o],
            device_id=to, device_id_type=MESH,
        )

    for which in range(2):
        for o in (2, 1, 3):
            qkv_copy(which, o, y).start()
    qs[x] = head_norm(part[1, :, 0:HD], qg_ref[...])
    for o in (2, 1, 3):
        qkv_copy(2, o, x).start()
    wo_step(6)
    for which in range(2):
        for o in (1, 3, 2):
            qkv_copy(which, o, (y + 4 - o) % 4).wait_recv()
    for o in (1, 3, 2):
        qkv_copy(2, o, (x + 4 - o) % 4).wait_recv()

    def nd_copy(which, o):
        src, dst = ((nsend, nrecv), (dsend, drecv))[which]
        return pltpu.make_async_remote_copy(
            src_ref=src.at[o], dst_ref=dst.at[o],
            send_sem=nd_s.at[which, o], recv_sem=nd_r.at[which, o],
            device_id=at((x + o) % 4, y), device_id_type=MESH,
        )

    def attend(queries):
        top = jnp.zeros((HD, NT), F32)
        low = jnp.zeros((1, NT), F32)
        for j in range(4):
            scores = lax.dot_general(
                ks[j], queries, (((1,), (1,)), ((), ())), preferred_element_type=F32
            ) * HD ** (-0.5)
            probs = jnp.exp(scores) * mask[...]
            low = low + jnp.sum(probs, axis=0, keepdims=True)
            top = top + dot(vs[j], probs.astype(BF))
        return top, low

    for o in (2, 1, 3):
        top, low = attend(qs[(x + o) % 4])
        nsend[o] = top.astype(BF)
        dsend[o] = jnp.broadcast_to(low, (8, NT))
        nd_copy(0, o).start()
        nd_copy(1, o).start()
        if o == 1:
            wo_step(7)
    top, low = attend(qs[x])
    wo_step(8)
    for o in (2, 1, 3):
        nd_copy(0, o).wait_recv()
        nd_copy(1, o).wait_recv()
        top = top + nrecv[o].astype(F32)
        low = low + drecv[o][0:1, :]
    asend[...] = jnp.transpose(top / low).reshape(2, NZ, 8, HD).astype(BF)

    home_y, home_x = gw.place(z)
    home = home_y * 4 + home_x
    slot = x * 4 + y

    def aa_copy(side, o):
        way = jnp.where(side == core, 0, 1)
        return pltpu.make_async_remote_copy(
            src_ref=asend.at[side, (z + o) % NZ], dst_ref=brecv.at[slot, core],
            send_sem=aa_s.at[way, o], recv_sem=aa_r.at[core, slot],
            device_id=((z + o) % NZ, home * 2 + side), device_id_type=MESH,
        )

    def aa_arrival(side, i):
        return pltpu.make_async_remote_copy(
            src_ref=asend.at[core, z], dst_ref=brecv.at[i, side],
            send_sem=aa_s.at[0, 0], recv_sem=aa_r.at[side, i],
            device_id=(gw.mine, ((i % 4) * 4 + i // 4) * 2 + side), device_id_type=MESH,
        )

    for o in FAR_FIRST:
        aa_copy(core, o).start()
        aa_copy(1 - core, o).start()
    aa_copy(1 - core, 0).start()

    @pl.when(home != chip)
    def _():
        aa_copy(core, 0).start()

    @pl.when(home == chip)
    def _():
        brecv[slot, core] = asend[core, z]

    for o in range(NZ):
        wo_sib(1 - core, o).wait_recv()
    for i in range(NZ):
        aa_arrival(1 - core, i).wait_recv()

        @pl.when((home != chip) | (slot != i))
        def _(i=i):
            aa_arrival(core, i).wait_recv()

    rows = [brecv[:, k].astype(F32).reshape(HALF, HD).astype(BF) for k in range(2)]
    rows = jnp.concatenate(rows, axis=1)

    def sum_copy(phase, half, p, o):
        along_x = (half == 0) == (phase == 0)
        to = at((x + o) % 4, y) if along_x else at(x, (y + o) % 4)
        slot = ((x if along_x else y) + o) % 4
        src, dst, ss, sr = ((ts, tr, t_s, t_r), (us, ur, u_s, u_r))[phase]
        return pltpu.make_async_remote_copy(
            src_ref=src.at[half, p, slot], dst_ref=dst.at[half, p, o],
            send_sem=ss.at[half, p, o], recv_sem=sr.at[half, p, o],
            device_id=to, device_id_type=MESH,
        )

    per = WIDE // BLK
    for p in range(PIECES):
        for half in range(2):
            for i in range(per):
                j = half * 8 + p * per + i
                cols = slice(i * BLK, (i + 1) * BLK)
                term = dot(rows, jnp.concatenate([wog[0, j], wog[1, j]], axis=0))
                term = term.reshape(4, 4, 8, BLK)
                for q in range(4):
                    mine = term[q] if half == 0 else term[:, q]
                    ts[half, p, q, :, cols] = mine.reshape(32, BLK).astype(BF)
            for o in (2, 1, 3):
                sum_copy(0, half, p, o).start()
    for p in range(PIECES):
        for half in range(2):
            total = ts[half, p, x if half == 0 else y].astype(F32)
            for o in (1, 3, 2):
                sum_copy(0, half, p, o).wait_recv()
                total = total + tr[half, p, o].astype(F32)
            us[half, p] = total.reshape(4, 8, WIDE).astype(BF)
            for o in (2, 1, 3):
                sum_copy(1, half, p, o).start()

    for o in range(1, NZ):
        x_copy(o).wait_send()
    x_sib(core).wait_send()
    gw.drain()
    for way in range(2):
        for t in range(8):
            wo_copy(way, t).wait_send()
            for p in range(2):
                if t > 0 or p == way:
                    rs_copy(way, t, p).wait_send()
    for o in range(NZ):
        wo_sib(core, o).wait_send()
        aa_copy(1 - core, o).wait_send()
        if o > 0:
            aa_copy(core, o).wait_send()

    @pl.when(home != chip)
    def _():
        aa_copy(core, 0).wait_send()

    for o in (1, 2, 3):
        for which in range(3):
            qkv_copy(which, o, y if which < 2 else x).wait_send()
        for which in range(2):
            nd_copy(which, o).wait_send()
        for half in range(2):
            for p in range(PIECES):
                sum_copy(0, half, p, o).wait_send()

    for p in range(PIECES):
        for half in range(2):
            total = us[half, p, y if half == 0 else x].astype(F32)
            for o in (1, 3, 2):
                sum_copy(1, half, p, o).wait_recv()
                total = total + ur[half, p, o].astype(F32)
            first = half * 8 * BLK + p * WIDE
            out_ref[:, first:first + WIDE] = total.astype(BF)
    for o in (1, 2, 3):
        for half in range(2):
            for p in range(PIECES):
                sum_copy(1, half, p, o).wait_send()


def body(latents, levels, order, level_table, q_gain, k_gain, w_qkv, w_out):
    vmem = pl.BlockSpec(memory_space=pltpu.VMEM)
    smem = pl.BlockSpec(memory_space=pltpu.SMEM)
    hbm = pl.BlockSpec(memory_space=pl.ANY)
    dma = pltpu.SemaphoreType.DMA
    return pl.pallas_call(
        kernel,
        out_shape=jax.ShapeDtypeStruct(latents.shape, BF),
        in_specs=[hbm, smem, smem, hbm, hbm, hbm, hbm, hbm],
        out_specs=vmem,
        scratch_shapes=[
            pltpu.VMEM(latents.shape, BF),
            pltpu.VMEM(level_table.shape, F32),
            pltpu.VMEM((1, HD), F32),
            pltpu.VMEM((1, HD), F32),
            pltpu.VMEM((16, BLK, BLK), BF),
            pltpu.VMEM((NZ, 8, BLK), BF),
            pltpu.VMEM((2, NZ, 8, BLK), BF),
            pltpu.VMEM((NT, BLK), BF),
            pltpu.VMEM((2, NT, BLK), F32),
            pltpu.VMEM((2, 8, NT, BLK), BF),
            pltpu.VMEM((2, 8, NT, BLK), BF),
            pltpu.VMEM((NT, NT), F32),
            pltpu.VMEM((4, NT, HD), BF),
            pltpu.VMEM((4, NT, HD), BF),
            pltpu.VMEM((4, HD, NT), BF),
            pltpu.VMEM((4, HD, NT), BF),
            pltpu.VMEM((4, HD, NT), BF),
            pltpu.VMEM((4, 8, NT), F32),
            pltpu.VMEM((4, 8, NT), F32),
            pltpu.VMEM((2, NZ, HD, BLK), BF),
            pltpu.VMEM((2, NZ, 8, HD), BF),
            pltpu.VMEM((NZ, 2, 8, HD), BF),
            pltpu.VMEM((2, PIECES, 4, 32, WIDE), BF),
            pltpu.VMEM((2, PIECES, 4, 32, WIDE), BF),
            pltpu.VMEM((2, PIECES, 4, 8, WIDE), BF),
            pltpu.VMEM((2, PIECES, 4, 8, WIDE), BF),
            dma((6,)),
            dma((NZ,)), dma((NZ,)),
            dma((1,)), dma((1,)),
            dma((2, 3)), dma((2, 4, 3)), dma((2, 16)),
            dma((2, 8)), dma((2, 8)),
            dma((NZ,)), dma((NZ,)),
            dma((2, 8, 2)), dma((2, 8, 2)),
            dma((3, 4)), dma((3, 4)),
            dma((2, 4)), dma((2, 4)),
            dma((2, NZ)), dma((2, NZ)),
            dma((2, PIECES, 4)), dma((2, PIECES, 4)),
            dma((2, PIECES, 4)), dma((2, PIECES, 4)),
        ],
        compiler_params=pltpu.CompilerParams(
            collective_id=0, has_side_effects=True, vmem_limit_bytes=60 * 2**20
        ),
        name="spans",
    )(
        latents, levels, order, level_table,
        q_gain.reshape(1, HD), k_gain.reshape(1, HD), w_qkv, w_out,
    )


def solution(mesh):
    placed = (
        P(("span", "seq"), None),
        P("span"),
        P(),
        P(),
        P(),
        P(),
        P("span", "seq"),
        P("seq", "span"),
    )
    return jax.shard_map(
        body, mesh=mesh, in_specs=placed, out_specs=P(("span", "seq"), None), check_vma=False
    )
```

```python
import jax
import jax.numpy as jnp
from jax import lax
from jax.experimental import pallas as pl
from jax.experimental.pallas import tpu as pltpu
from jax.sharding import PartitionSpec as P

HD = 128
NZ = 16
BF = jnp.bfloat16
F32 = jnp.float32
MESH = pl.DeviceIdType.MESH
BLK = 384
NT = 256
HALF = 128
FAR_FIRST = (8, 7, 9, 6, 10, 5, 11, 4, 12, 3, 13, 2, 14, 1, 15)
FIRST = 6
PARTS = 1
WO_AT = {0: 3, 3: 4, 6: 5}
PIECES = 2
WIDE = 8 * BLK // PIECES


def dot(a, b):
    return jnp.dot(a, b, preferred_element_type=F32)


def take(ref, sem):
    pltpu.make_async_copy(ref, ref, sem).wait()


class PlaneGather:
    def __init__(self, buf, rows, x, y, at, s1, rs):
        self.buf, self.rows, self.x, self.y, self.at = buf, rows, x, y, at
        self.s1, self.rs = s1, rs
        self.mine = ((x + 4 - y) % 4) * 4 + y

    @staticmethod
    def place(block):
        return block % 4, (block + block // 4) % 4

    def part(self, block, half, part):
        rows = self.rows // PARTS
        return self.buf.at[block, pl.ds(half * self.rows + part * rows, rows)]

    def target(self, half, phase, o):
        along_x = (half == 0) == (phase == 1)
        if along_x:
            return self.at((self.x + o) % 4, self.y)
        return self.at(self.x, (self.y + o) % 4)

    def copy(self, block, half, part, phase, i):
        o = (1, 3, 2)[i]
        sem = self.s1.at[phase - 1, half, i]
        ref = self.part(block, half, part)
        return pltpu.make_async_remote_copy(
            src_ref=ref,
            dst_ref=ref,
            send_sem=sem,
            recv_sem=self.rs.at[half, part, block],
            device_id=self.target(half, phase, o),
            device_id_type=MESH,
        )

    def first(self):
        for part in range(PARTS):
            for i in range(3):
                for half in range(2):
                    self.copy(self.mine, half, part, 1, i).start()

    def wait_block(self, block, half, part):
        self.copy(block, half, part, 1, 0).wait_recv()

    def second(self, block, part):
        by, bx = self.place(block)
        for half in range(2):
            same = (by == self.y) if half == 0 else (bx == self.x)

            @pl.when(same)
            def _(half=half):
                @pl.when(block != self.mine)
                def _():
                    self.wait_block(block, half, part)

                for i in range(3):
                    self.copy(block, half, part, 2, i).start()

    def use(self, block):
        by, bx = self.place(block)

        @pl.when(by != self.y)
        def _():
            for part in range(PARTS):
                self.wait_block(block, 0, part)

        @pl.when(bx != self.x)
        def _():
            for part in range(PARTS):
                self.wait_block(block, 1, part)

    def drain(self):
        for half in range(2):
            for i in range(3):
                self.copy(self.mine, half, 0, 1, i).wait_send()
                take(self.buf.at[pl.ds(0, 2)], self.s1.at[1, half, i])


def kernel(
    lat_hbm, lev_ref, ord_ref, tab_hbm, qg_hbm, kg_hbm, w_ref, wo_ref, out_ref,
    lat_ref, tab_ref, qg_ref, kg_ref, wall, xsend, xr, xin, part, cws, cwr, mask,
    qs, ks, vs, nsend, nrecv, dsend, drecv, tops, lows, wog, asend, brecv, ts, tr, us, ur,
    load_sem, xa_s, xa_r, sib_s, sib_r, w1, wr, wo_s, wo_r, ws_s, ws_r,
    rs_s, rs_r, qkv_s, qkv_r, nd_s, nd_r, aa_s, aa_r, t_s, t_r, u_s, u_r,
):
    z = lax.axis_index("span")
    s = lax.axis_index("seq")
    core = s % 2
    chip = s // 2
    x = chip % 4
    y = chip // 4

    def at(px, py):
        return (z, (py * 4 + px) * 2 + core)

    def along_z(o):
        return ((z + o) % NZ, s)

    sibling = (z, chip * 2 + 1 - core)

    gw = PlaneGather(wall, BLK // 2, x, y, at, w1, wr)
    loads = [
        pltpu.make_async_copy(src, dst, load_sem.at[i])
        for i, (src, dst) in enumerate((
            (lat_hbm, lat_ref), (tab_hbm, tab_ref), (w_ref, wall.at[gw.mine]),
            (wo_ref, wog.at[core, z]), (qg_hbm, qg_ref), (kg_hbm, kg_ref),
        ))
    ]
    for load in loads:
        load.start()

    barrier = pltpu.get_barrier_semaphore()
    for o in FAR_FIRST:
        pl.semaphore_signal(barrier, inc=1, device_id=along_z(o), device_id_type=MESH)
    for o in (2, 1, 3):
        pl.semaphore_signal(barrier, inc=1, device_id=at((x + o) % 4, y), device_id_type=MESH)
        pl.semaphore_signal(barrier, inc=1, device_id=at(x, (y + o) % 4), device_id_type=MESH)
    pl.semaphore_signal(barrier, inc=1, device_id=sibling, device_id_type=MESH)

    for load in loads:
        load.wait()
    width = lat_ref.shape[1]
    level = lev_ref[0]
    row = tab_ref[pl.ds(level, 1), :]
    values = lat_ref[...].astype(F32)
    center = values - jnp.mean(values, axis=1, keepdims=True)
    spread = jnp.mean(center * center, axis=1, keepdims=True)
    modulated = center * lax.rsqrt(spread + 1e-06) * (1.0 + row[:, width:]) + row[:, :width]
    modulated = modulated.astype(BF)
    for j in range(NZ):
        xsend[j] = modulated[:, j * BLK:(j + 1) * BLK]
    xr[core, z] = xsend[z]

    def wo_copy(way, t, arrival=False):
        back = t + (1 if arrival else 0)
        slot = (z + NZ - back) % NZ if way == 0 else (z + back) % NZ
        ref = wog.at[core, slot]
        if t == 7:
            ref = wog.at[core, slot, pl.ds(way * (HD // 2), HD // 2)]
        return pltpu.make_async_remote_copy(
            src_ref=ref, dst_ref=ref,
            send_sem=wo_s.at[0], recv_sem=wo_r.at[way, t],
            device_id=along_z(1 if way == 0 else NZ - 1), device_id_type=MESH,
        )

    def wo_sib(side, o):
        ref = wog.at[side, (z + o) % NZ]
        return pltpu.make_async_remote_copy(
            src_ref=ref, dst_ref=ref, send_sem=ws_s.at[0], recv_sem=ws_r.at[0],
            device_id=sibling, device_id_type=MESH,
        )

    def wo_step(t):
        if t > 0:
            for way in range(2):
                wo_copy(way, t - 1, True).wait_recv()
        if t < 8:
            for way in range(2):
                wo_copy(way, t).start()
        if t == 0 or t == 8:
            wo_sib(core, t).start()
        else:
            wo_sib(core, t).start()
            wo_sib(core, NZ - t).start()

    def x_copy(o):
        return pltpu.make_async_remote_copy(
            src_ref=xsend.at[(z + o) % NZ], dst_ref=xr.at[core, z],
            send_sem=xa_s.at[0], recv_sem=xa_r.at[0],
            device_id=along_z(o), device_id_type=MESH,
        )

    pl.semaphore_wait(barrier, 22)
    gw.first()

    for o in FAR_FIRST:
        x_copy(o).start()
    wo_step(0)

    key_span = (lax.broadcasted_iota(jnp.int32, (NT, HD), 0) % HALF) // 8
    query_span = (lax.broadcasted_iota(jnp.int32, (8, NT), 1) % HALF) // 8
    key_order = jnp.zeros((NT, HD), jnp.int32)
    query_order = jnp.zeros((8, NT), jnp.int32)
    for j in range(NZ):
        place = ord_ref[j]
        key_order = jnp.where(key_span == j, place, key_order)
        query_order = jnp.where(query_span == j, place, query_order)
    key_order = jnp.concatenate([key_order, key_order], axis=1)
    mask[...] = jnp.where(key_order <= query_order[0:1, :], 1.0, 0.0)

    take(xr.at[core, pl.ds(0, NZ - 1)], xa_r.at[0])

    def x_sib(slot):
        return pltpu.make_async_remote_copy(
            src_ref=xr.at[slot], dst_ref=xr.at[slot],
            send_sem=sib_s.at[0], recv_sem=sib_r.at[0],
            device_id=sibling, device_id_type=MESH,
        )

    x_sib(core).start()

    def place_of(t, way):
        return (z + 8 - t) % NZ if way == 0 else (z + 8 + t) % NZ

    order_of_use = [place_of(0, 0)]
    for t in range(1, 8):
        order_of_use += [place_of(t, 0), place_of(t, 1)]
    order_of_use.append(z)
    for piece in range(PARTS):
        for block in order_of_use[:FIRST]:
            gw.second(block, piece)

    wo_step(1)
    x_sib(1 - core).wait_recv()
    xin[...] = xr[...].astype(F32).reshape(NT, BLK).astype(BF)

    wo_step(2)

    def rs_copy(way, t, p):
        rows = pl.ds(p * HALF, HALF)
        return pltpu.make_async_remote_copy(
            src_ref=cws.at[way, t, rows], dst_ref=cwr.at[way, t, rows],
            send_sem=rs_s.at[way], recv_sem=rs_r.at[way, t, p],
            device_id=along_z(1 if way == 0 else NZ - 1), device_id_type=MESH,
        )

    for t in range(8):
        if t == 0:
            block = place_of(0, 0)
            gw.use(block)
            cws[0, 0, 0:HALF] = dot(xin[0:HALF], wall[block]).astype(BF)
            rs_copy(0, 0, 0).start()
            cws[1, 0, HALF:NT] = dot(xin[HALF:NT], wall[block]).astype(BF)
            rs_copy(1, 0, 1).start()
        else:
            for way in range(2):
                block = place_of(t, way)
                gw.use(block)
                part[way] = dot(xin[...], wall[block])
            for p in range(2):
                rows = slice(p * HALF, (p + 1) * HALF)
                for way in range(2):
                    total = part[way, rows]
                    if t > 1 or p == way:
                        rs_copy(way, t - 1, p).wait_recv()
                        total = total + cwr[way, t - 1, rows].astype(F32)
                    cws[way, t, rows] = total.astype(BF)
                    rs_copy(way, t, p).start()
        for block in order_of_use[FIRST + 2 * t:FIRST + 2 * t + 2]:
            for piece in range(PARTS):
                gw.second(block, piece)
        if t in WO_AT:
            wo_step(WO_AT[t])
    gw.use(z)
    part[0] = dot(xin[...], wall[z])

    def head_norm(block, gain):
        square = jnp.mean(block * block, axis=-1, keepdims=True)
        return (block * lax.rsqrt(square + 1e-06) * gain).astype(BF)

    def qkv_copy(which, o, p, me):
        ref = (ks, vs, qs)[which].at[me]
        half = pl.ds(p * HALF, HALF)
        ref = ref.at[:, half] if which == 1 else ref.at[half]
        to = at(x, (y + o) % 4) if which < 2 else at((x + o) % 4, y)
        return pltpu.make_async_remote_copy(
            src_ref=ref, dst_ref=ref,
            send_sem=qkv_s.at[0], recv_sem=qkv_r.at[which, o],
            device_id=to, device_id_type=MESH,
        )

    for p in range(2):
        rows = slice(p * HALF, (p + 1) * HALF)
        for way in range(2):
            rs_copy(way, 7, p).wait_recv()
        total = part[0, rows] + cwr[0, 7, rows].astype(F32) + cwr[1, 7, rows].astype(F32)
        total = total.astype(BF).astype(F32)
        ks[y, rows] = head_norm(total[:, HD:2 * HD], kg_ref[...])
        vs[y, :, rows] = jnp.transpose(total[:, 2 * HD:3 * HD]).astype(BF)
        for o in (2, 1, 3):
            for which in range(2):
                qkv_copy(which, o, p, y).start()
        qs[x, rows] = head_norm(total[:, 0:HD], qg_ref[...])
        for o in (2, 1, 3):
            qkv_copy(2, o, p, x).start()
    wo_step(6)
    def nd_copy(which, o):
        src, dst = ((nsend, nrecv), (dsend, drecv))[which]
        return pltpu.make_async_remote_copy(
            src_ref=src.at[o], dst_ref=dst.at[o],
            send_sem=nd_s.at[which], recv_sem=nd_r.at[which, o],
            device_id=at((x + o) % 4, y), device_id_type=MESH,
        )

    def attend(first, j, o):
        queries = qs[(x + o) % 4]
        scores = lax.dot_general(
            ks[j], queries, (((1,), (1,)), ((), ())), preferred_element_type=F32
        ) * HD ** (-0.5)
        probs = jnp.exp(scores) * mask[...]
        low = jnp.sum(probs, axis=0, keepdims=True)
        top = dot(vs[j], probs.astype(BF))
        if not first:
            low = low + lows[o]
            top = top + tops[o]
        return top, low

    def attend_all(first, j):
        for o in range(4):
            tops[o], lows[o] = attend(first, j, o)

    tops[0], lows[0] = attend(True, y, 0)
    for o in (1, 3, 2):
        take(qs.at[(x + 4 - o) % 4], qkv_r.at[2, o])
        tops[4 - o], lows[4 - o] = attend(True, y, 4 - o)
    for o in (1, 3):
        take(ks.at[(y + 4 - o) % 4], qkv_r.at[0, o])
        take(vs.at[(y + 4 - o) % 4], qkv_r.at[1, o])
        attend_all(False, (y + 4 - o) % 4)
        if o == 1:
            wo_step(7)
    take(ks.at[(y + 2) % 4], qkv_r.at[0, 2])
    take(vs.at[(y + 2) % 4], qkv_r.at[1, 2])
    for o in (2, 1, 3):
        top, low = attend(False, (y + 2) % 4, o)
        nsend[o] = top.astype(BF)
        dsend[o] = jnp.broadcast_to(low, (8, NT))
        nd_copy(0, o).start()
        nd_copy(1, o).start()
    top, low = attend(False, (y + 2) % 4, 0)
    wo_step(8)
    for o in (2, 1, 3):
        nd_copy(0, o).wait_recv()
        nd_copy(1, o).wait_recv()
        top = top + nrecv[o].astype(F32)
        low = low + drecv[o][0:1, :]
    asend[...] = jnp.transpose(top / low).reshape(2, NZ, 8, HD).astype(BF)

    home_y, home_x = gw.place(z)
    home = home_y * 4 + home_x
    slot = x * 4 + y

    def aa_copy(side, o):
        way = 0 if side is core else 1
        return pltpu.make_async_remote_copy(
            src_ref=asend.at[side, (z + o) % NZ], dst_ref=brecv.at[core, slot],
            send_sem=aa_s.at[way], recv_sem=aa_r.at[core],
            device_id=((z + o) % NZ, home * 2 + side), device_id_type=MESH,
        )

    for o in FAR_FIRST:
        aa_copy(core, o).start()
        aa_copy(1 - core, o).start()
    aa_copy(1 - core, 0).start()

    @pl.when(home != chip)
    def _():
        aa_copy(core, 0).start()

    @pl.when(home == chip)
    def _():
        brecv[core, slot] = asend[core, z]

    take(wog.at[1 - core], ws_r.at[0])
    take(brecv.at[1 - core], aa_r.at[1 - core])

    @pl.when((home != chip) | (gw.mine != z))
    def _():
        take(brecv.at[core], aa_r.at[core])

    @pl.when((home == chip) & (gw.mine == z))
    def _():
        take(brecv.at[core, pl.ds(0, NZ - 1)], aa_r.at[core])

    rows = [brecv[k].astype(F32).reshape(HALF, HD).astype(BF) for k in range(2)]
    rows = jnp.concatenate(rows, axis=1)

    def sum_copy(phase, half, p, o):
        along_x = (half == 0) == (phase == 0)
        to = at((x + o) % 4, y) if along_x else at(x, (y + o) % 4)
        slot = ((x if along_x else y) + o) % 4
        src, dst, ss, sr = ((ts, tr, t_s, t_r), (us, ur, u_s, u_r))[phase]
        return pltpu.make_async_remote_copy(
            src_ref=src.at[half, p, slot], dst_ref=dst.at[half, p, o],
            send_sem=ss.at[half, p], recv_sem=sr.at[half, p],
            device_id=to, device_id_type=MESH,
        )

    per = WIDE // BLK
    for p in range(PIECES):
        for half in range(2):
            for i in range(per):
                j = half * 8 + p * per + i
                cols = slice(i * BLK, (i + 1) * BLK)
                term = dot(rows, jnp.concatenate([wog[0, j], wog[1, j]], axis=0))
                term = term.reshape(4, 4, 8, BLK)
                for q in range(4):
                    mine = term[q] if half == 0 else term[:, q]
                    ts[half, p, q, :, cols] = mine.reshape(32, BLK).astype(BF)
            for o in (2, 1, 3):
                sum_copy(0, half, p, o).start()
    for p in range(PIECES):
        for half in range(2):
            total = ts[half, p, x if half == 0 else y].astype(F32)
            take(tr.at[half, p, pl.ds(1, 3)], t_r.at[half, p])
            for o in (1, 2, 3):
                total = total + tr[half, p, o].astype(F32)
            us[half, p] = total.reshape(4, 8, WIDE).astype(BF)
            for o in (2, 1, 3):
                sum_copy(1, half, p, o).start()

    take(xsend.at[pl.ds(0, NZ - 1)], xa_s.at[0])
    x_sib(core).wait_send()
    gw.drain()
    take(wall.at[pl.ds(0, 5)], rs_s.at[0])
    take(wall.at[pl.ds(0, 5)], rs_s.at[1])
    take(wall.at[pl.ds(0, 5)], wo_s.at[0])
    take(wog.at[core], ws_s.at[0])
    take(wall.at[pl.ds(0, 2)], qkv_s.at[0])
    take(nsend.at[pl.ds(1, 3)], nd_s.at[0])
    take(dsend.at[pl.ds(1, 3)], nd_s.at[1])
    take(asend.at[1 - core], aa_s.at[1])

    @pl.when(home != chip)
    def _():
        take(asend.at[core], aa_s.at[0])

    @pl.when(home == chip)
    def _():
        take(asend.at[core, pl.ds(0, NZ - 1)], aa_s.at[0])

    for p in range(PIECES):
        for half in range(2):
            take(ts.at[half, p, pl.ds(0, 3)], t_s.at[half, p])

    for p in range(PIECES):
        for half in range(2):
            total = us[half, p, y if half == 0 else x].astype(F32)
            take(ur.at[half, p, pl.ds(1, 3)], u_r.at[half, p])
            for o in (1, 2, 3):
                total = total + ur[half, p, o].astype(F32)
            first = half * 8 * BLK + p * WIDE
            out_ref[:, first:first + WIDE] = total.astype(BF)
    for p in range(PIECES):
        for half in range(2):
            take(us.at[half, p, pl.ds(0, 3)], u_s.at[half, p])


def body(latents, levels, order, level_table, q_gain, k_gain, w_qkv, w_out):
    vmem = pl.BlockSpec(memory_space=pltpu.VMEM)
    smem = pl.BlockSpec(memory_space=pltpu.SMEM)
    hbm = pl.BlockSpec(memory_space=pl.ANY)
    dma = pltpu.SemaphoreType.DMA
    return pl.pallas_call(
        kernel,
        out_shape=jax.ShapeDtypeStruct(latents.shape, BF),
        in_specs=[hbm, smem, smem, hbm, hbm, hbm, hbm, hbm],
        out_specs=vmem,
        scratch_shapes=[
            pltpu.VMEM(latents.shape, BF),
            pltpu.VMEM(level_table.shape, F32),
            pltpu.VMEM((1, HD), F32),
            pltpu.VMEM((1, HD), F32),
            pltpu.VMEM((16, BLK, BLK), BF),
            pltpu.VMEM((NZ, 8, BLK), BF),
            pltpu.VMEM((2, NZ, 8, BLK), BF),
            pltpu.VMEM((NT, BLK), BF),
            pltpu.VMEM((2, NT, BLK), F32),
            pltpu.VMEM((2, 8, NT, BLK), BF),
            pltpu.VMEM((2, 8, NT, BLK), BF),
            pltpu.VMEM((NT, NT), F32),
            pltpu.VMEM((4, NT, HD), BF),
            pltpu.VMEM((4, NT, HD), BF),
            pltpu.VMEM((4, HD, NT), BF),
            pltpu.VMEM((4, HD, NT), BF),
            pltpu.VMEM((4, HD, NT), BF),
            pltpu.VMEM((4, 8, NT), F32),
            pltpu.VMEM((4, 8, NT), F32),
            pltpu.VMEM((4, HD, NT), F32),
            pltpu.VMEM((4, 1, NT), F32),
            pltpu.VMEM((2, NZ, HD, BLK), BF),
            pltpu.VMEM((2, NZ, 8, HD), BF),
            pltpu.VMEM((2, NZ, 8, HD), BF),
            pltpu.VMEM((2, PIECES, 4, 32, WIDE), BF),
            pltpu.VMEM((2, PIECES, 4, 32, WIDE), BF),
            pltpu.VMEM((2, PIECES, 4, 8, WIDE), BF),
            pltpu.VMEM((2, PIECES, 4, 8, WIDE), BF),
            dma((6,)),
            dma((1,)), dma((1,)),
            dma((1,)), dma((1,)),
            dma((2, 2, 3)), dma((2, PARTS, 16)),
            dma((1,)), dma((2, 8)),
            dma((1,)), dma((1,)),
            dma((2,)), dma((2, 8, 2)),
            dma((1,)), dma((3, 4)),
            dma((2,)), dma((2, 4)),
            dma((2,)), dma((2,)),
            dma((2, PIECES)), dma((2, PIECES)),
            dma((2, PIECES)), dma((2, PIECES)),
        ],
        compiler_params=pltpu.CompilerParams(
            collective_id=0, has_side_effects=True, vmem_limit_bytes=60 * 2**20
        ),
        name="spans",
    )(
        latents, levels, order, level_table,
        q_gain.reshape(1, HD), k_gain.reshape(1, HD), w_qkv, w_out,
    )


def solution(mesh):
    placed = (
        P(("span", "seq"), None),
        P("span"),
        P(),
        P(),
        P(),
        P(),
        P("span", "seq"),
        P("seq", "span"),
    )
    return jax.shard_map(
        body, mesh=mesh, in_specs=placed, out_specs=P(("span", "seq"), None), check_vma=False
    )
```

```python
import jax
import jax.numpy as jnp
from jax import lax
from jax.experimental import pallas as pl
from jax.experimental.pallas import tpu as pltpu
from jax.sharding import PartitionSpec as P

HD = 128
NZ = 16
BF = jnp.bfloat16
F32 = jnp.float32
MESH = pl.DeviceIdType.MESH
BLK = 384
NT = 256
HALF = 128
FAR_FIRST = (8, 7, 9, 6, 10, 5, 11, 4, 12, 3, 13, 2, 14, 1, 15)
FIRST = 6
PARTS = 1
WO_AT = {0: 3, 5: 4}
PIECES = 2
WIDE = 8 * BLK // PIECES


def dot(a, b):
    return jnp.dot(a, b, preferred_element_type=F32)


def take(ref, sem):
    pltpu.make_async_copy(ref, ref, sem).wait()


class PlaneGather:
    def __init__(self, buf, rows, x, y, at, s1, rs):
        self.buf, self.rows, self.x, self.y, self.at = buf, rows, x, y, at
        self.s1, self.rs = s1, rs
        self.mine = ((x + 4 - y) % 4) * 4 + y

    @staticmethod
    def place(block):
        return block % 4, (block + block // 4) % 4

    def part(self, block, half, part):
        rows = self.rows // PARTS
        return self.buf.at[block, pl.ds(half * self.rows + part * rows, rows)]

    def target(self, half, phase, o):
        along_x = (half == 0) == (phase == 1)
        if along_x:
            return self.at((self.x + o) % 4, self.y)
        return self.at(self.x, (self.y + o) % 4)

    def copy(self, block, half, part, phase, i):
        o = (1, 3, 2)[i]
        sem = self.s1.at[phase - 1, half, i]
        ref = self.part(block, half, part)
        return pltpu.make_async_remote_copy(
            src_ref=ref,
            dst_ref=ref,
            send_sem=sem,
            recv_sem=self.rs.at[half, part, block],
            device_id=self.target(half, phase, o),
            device_id_type=MESH,
        )

    def first(self):
        for part in range(PARTS):
            for i in range(3):
                for half in range(2):
                    self.copy(self.mine, half, part, 1, i).start()

    def wait_block(self, block, half, part):
        self.copy(block, half, part, 1, 0).wait_recv()

    def second(self, block, part):
        by, bx = self.place(block)
        for half in range(2):
            same = (by == self.y) if half == 0 else (bx == self.x)

            @pl.when(same)
            def _(half=half):
                @pl.when(block != self.mine)
                def _():
                    self.wait_block(block, half, part)

                for i in range(3):
                    self.copy(block, half, part, 2, i).start()

    def use(self, block):
        by, bx = self.place(block)

        @pl.when(by != self.y)
        def _():
            for part in range(PARTS):
                self.wait_block(block, 0, part)

        @pl.when(bx != self.x)
        def _():
            for part in range(PARTS):
                self.wait_block(block, 1, part)

    def drain(self):
        for half in range(2):
            for i in range(3):
                self.copy(self.mine, half, 0, 1, i).wait_send()
                take(self.buf.at[pl.ds(0, 2)], self.s1.at[1, half, i])


def kernel(
    lat_hbm, lev_ref, ord_ref, tab_hbm, qg_hbm, kg_hbm, w_ref, wo_ref, out_ref,
    lat_ref, tab_ref, qg_ref, kg_ref, wall, xsend, xr, xin, part, cws, cwr, mask,
    qs, ks, vs, nsend, nrecv, dsend, drecv, tops, lows, wog, asend, brecv, ts, tr, us, ur,
    load_sem, xa_s, xa_r, sib_s, sib_r, w1, wr, wo_s, wo_r, ws_s, ws_r,
    rs_s, rs_r, qkv_s, qkv_r, nd_s, nd_r, aa_s, aa_r, t_s, t_r, u_s, u_r,
):
    z = lax.axis_index("span")
    s = lax.axis_index("seq")
    core = s % 2
    chip = s // 2
    x = chip % 4
    y = chip // 4

    def at(px, py):
        return (z, (py * 4 + px) * 2 + core)

    def along_z(o):
        return ((z + o) % NZ, s)

    sibling = (z, chip * 2 + 1 - core)

    gw = PlaneGather(wall, BLK // 2, x, y, at, w1, wr)
    loads = [
        pltpu.make_async_copy(src, dst, load_sem.at[i])
        for i, (src, dst) in enumerate((
            (lat_hbm, lat_ref), (tab_hbm, tab_ref), (w_ref, wall.at[gw.mine]),
            (wo_ref, wog.at[core, z]), (qg_hbm, qg_ref), (kg_hbm, kg_ref),
        ))
    ]
    for load in loads:
        load.start()

    barrier = pltpu.get_barrier_semaphore()
    for o in FAR_FIRST:
        pl.semaphore_signal(barrier, inc=1, device_id=along_z(o), device_id_type=MESH)
    for o in (2, 1, 3):
        pl.semaphore_signal(barrier, inc=1, device_id=at((x + o) % 4, y), device_id_type=MESH)
        pl.semaphore_signal(barrier, inc=1, device_id=at(x, (y + o) % 4), device_id_type=MESH)
    pl.semaphore_signal(barrier, inc=1, device_id=sibling, device_id_type=MESH)

    for load in loads:
        load.wait()
    width = lat_ref.shape[1]
    level = lev_ref[0]
    row = tab_ref[pl.ds(level, 1), :]
    values = lat_ref[...].astype(F32)
    center = values - jnp.mean(values, axis=1, keepdims=True)
    spread = jnp.mean(center * center, axis=1, keepdims=True)
    modulated = center * lax.rsqrt(spread + 1e-06) * (1.0 + row[:, width:]) + row[:, :width]
    modulated = modulated.astype(BF)
    for j in range(NZ):
        xsend[j] = modulated[:, j * BLK:(j + 1) * BLK]
    xr[core, z] = xsend[z]

    def wo_copy(way, t, arrival=False):
        back = t + (1 if arrival else 0)
        slot = (z + NZ - back) % NZ if way == 0 else (z + back) % NZ
        ref = wog.at[core, slot]
        if t == 7:
            ref = wog.at[core, slot, pl.ds(way * (HD // 2), HD // 2)]
        return pltpu.make_async_remote_copy(
            src_ref=ref, dst_ref=ref,
            send_sem=wo_s.at[0], recv_sem=wo_r.at[way, t],
            device_id=along_z(1 if way == 0 else NZ - 1), device_id_type=MESH,
        )

    def wo_sib(side, o):
        ref = wog.at[side, (z + o) % NZ]
        return pltpu.make_async_remote_copy(
            src_ref=ref, dst_ref=ref, send_sem=ws_s.at[0], recv_sem=ws_r.at[0],
            device_id=sibling, device_id_type=MESH,
        )

    def wo_step(t):
        if t > 0:
            for way in range(2):
                wo_copy(way, t - 1, True).wait_recv()
        if t < 8:
            for way in range(2):
                wo_copy(way, t).start()
        if t == 0 or t == 8:
            wo_sib(core, t).start()
        else:
            wo_sib(core, t).start()
            wo_sib(core, NZ - t).start()

    def x_copy(o):
        return pltpu.make_async_remote_copy(
            src_ref=xsend.at[(z + o) % NZ], dst_ref=xr.at[core, z],
            send_sem=xa_s.at[0], recv_sem=xa_r.at[0],
            device_id=along_z(o), device_id_type=MESH,
        )

    pl.semaphore_wait(barrier, 22)
    gw.first()

    for o in FAR_FIRST:
        x_copy(o).start()
    wo_step(0)

    key_span = (lax.broadcasted_iota(jnp.int32, (NT, HD), 0) % HALF) // 8
    query_span = (lax.broadcasted_iota(jnp.int32, (8, NT), 1) % HALF) // 8
    key_order = jnp.zeros((NT, HD), jnp.int32)
    query_order = jnp.zeros((8, NT), jnp.int32)
    for j in range(NZ):
        place = ord_ref[j]
        key_order = jnp.where(key_span == j, place, key_order)
        query_order = jnp.where(query_span == j, place, query_order)
    key_order = jnp.concatenate([key_order, key_order], axis=1)
    mask[...] = jnp.where(key_order <= query_order[0:1, :], 1.0, 0.0)

    take(xr.at[core, pl.ds(0, NZ - 1)], xa_r.at[0])

    def x_sib(slot):
        return pltpu.make_async_remote_copy(
            src_ref=xr.at[slot], dst_ref=xr.at[slot],
            send_sem=sib_s.at[0], recv_sem=sib_r.at[0],
            device_id=sibling, device_id_type=MESH,
        )

    x_sib(core).start()

    def place_of(t, way):
        return (z + 8 - t) % NZ if way == 0 else (z + 8 + t) % NZ

    order_of_use = [place_of(0, 0)]
    for t in range(1, 8):
        order_of_use += [place_of(t, 0), place_of(t, 1)]
    order_of_use.append(z)
    for piece in range(PARTS):
        for block in order_of_use[:FIRST]:
            gw.second(block, piece)

    wo_step(1)
    x_sib(1 - core).wait_recv()
    xin[...] = xr[...].astype(F32).reshape(NT, BLK).astype(BF)

    wo_step(2)

    def rs_copy(way, t, p):
        rows = pl.ds(p * HALF, HALF)
        return pltpu.make_async_remote_copy(
            src_ref=cws.at[way, t, rows], dst_ref=cwr.at[way, t, rows],
            send_sem=rs_s.at[way], recv_sem=rs_r.at[way, t, p],
            device_id=along_z(1 if way == 0 else NZ - 1), device_id_type=MESH,
        )

    for t in range(8):
        if t == 0:
            block = place_of(0, 0)
            gw.use(block)
            cws[0, 0, 0:HALF] = dot(xin[0:HALF], wall[block]).astype(BF)
            rs_copy(0, 0, 0).start()
            cws[1, 0, HALF:NT] = dot(xin[HALF:NT], wall[block]).astype(BF)
            rs_copy(1, 0, 1).start()
        else:
            for way in range(2):
                block = place_of(t, way)
                gw.use(block)
                part[way] = dot(xin[...], wall[block])
            for p in range(2):
                rows = slice(p * HALF, (p + 1) * HALF)
                for way in range(2):
                    total = part[way, rows]
                    if t > 1 or p == way:
                        rs_copy(way, t - 1, p).wait_recv()
                        total = total + cwr[way, t - 1, rows].astype(F32)
                    cws[way, t, rows] = total.astype(BF)
                    rs_copy(way, t, p).start()
        for block in order_of_use[FIRST + 2 * t:FIRST + 2 * t + 2]:
            for piece in range(PARTS):
                gw.second(block, piece)
        if t in WO_AT:
            wo_step(WO_AT[t])
    gw.use(z)
    part[0] = dot(xin[...], wall[z])

    def head_norm(block, gain):
        square = jnp.mean(block * block, axis=-1, keepdims=True)
        return (block * lax.rsqrt(square + 1e-06) * gain).astype(BF)

    def qkv_copy(which, o, p, me):
        ref = (ks, vs, qs)[which].at[me]
        half = pl.ds(p * HALF, HALF)
        ref = ref.at[:, half] if which == 1 else ref.at[half]
        to = at(x, (y + o) % 4) if which < 2 else at((x + o) % 4, y)
        return pltpu.make_async_remote_copy(
            src_ref=ref, dst_ref=ref,
            send_sem=qkv_s.at[0], recv_sem=qkv_r.at[which, o],
            device_id=to, device_id_type=MESH,
        )

    for p in range(2):
        rows = slice(p * HALF, (p + 1) * HALF)
        for way in range(2):
            rs_copy(way, 7, p).wait_recv()
        total = part[0, rows] + cwr[0, 7, rows].astype(F32) + cwr[1, 7, rows].astype(F32)
        total = total.astype(BF).astype(F32)
        ks[y, rows] = head_norm(total[:, HD:2 * HD], kg_ref[...])
        vs[y, :, rows] = jnp.transpose(total[:, 2 * HD:3 * HD]).astype(BF)
        for o in (2, 1, 3):
            for which in range(2):
                qkv_copy(which, o, p, y).start()
        qs[x, rows] = head_norm(total[:, 0:HD], qg_ref[...])
        for o in (2, 1, 3):
            qkv_copy(2, o, p, x).start()
    wo_step(5)
    def nd_copy(which, o):
        src, dst = ((nsend, nrecv), (dsend, drecv))[which]
        return pltpu.make_async_remote_copy(
            src_ref=src.at[o], dst_ref=dst.at[o],
            send_sem=nd_s.at[which], recv_sem=nd_r.at[which, o],
            device_id=at((x + o) % 4, y), device_id_type=MESH,
        )

    def attend(first, j, o):
        queries = qs[(x + o) % 4]
        scores = lax.dot_general(
            ks[j], queries, (((1,), (1,)), ((), ())), preferred_element_type=F32
        ) * HD ** (-0.5)
        probs = jnp.exp(scores) * mask[...]
        low = jnp.sum(probs, axis=0, keepdims=True)
        top = dot(vs[j], probs.astype(BF))
        if not first:
            low = low + lows[o]
            top = top + tops[o]
        return top, low

    def attend_all(first, j):
        for o in range(4):
            tops[o], lows[o] = attend(first, j, o)

    tops[0], lows[0] = attend(True, y, 0)
    for o in (1, 3, 2):
        take(qs.at[(x + 4 - o) % 4], qkv_r.at[2, o])
        tops[4 - o], lows[4 - o] = attend(True, y, 4 - o)
    for o in (1, 3):
        take(ks.at[(y + 4 - o) % 4], qkv_r.at[0, o])
        take(vs.at[(y + 4 - o) % 4], qkv_r.at[1, o])
        attend_all(False, (y + 4 - o) % 4)
        if o == 1:
            wo_step(6)
    take(ks.at[(y + 2) % 4], qkv_r.at[0, 2])
    take(vs.at[(y + 2) % 4], qkv_r.at[1, 2])
    for o in (2, 1, 3):
        top, low = attend(False, (y + 2) % 4, o)
        nsend[o] = top.astype(BF)
        dsend[o] = jnp.broadcast_to(low, (8, NT))
        nd_copy(0, o).start()
        nd_copy(1, o).start()
    top, low = attend(False, (y + 2) % 4, 0)
    wo_step(7)
    for o in (2, 1, 3):
        nd_copy(0, o).wait_recv()
        nd_copy(1, o).wait_recv()
        top = top + nrecv[o].astype(F32)
        low = low + drecv[o][0:1, :]
    asend[...] = jnp.transpose(top / low).reshape(2, NZ, 8, HD).astype(BF)

    home_y, home_x = gw.place(z)
    home = home_y * 4 + home_x
    slot = x * 4 + y

    def aa_copy(side, o):
        way = 0 if side is core else 1
        return pltpu.make_async_remote_copy(
            src_ref=asend.at[side, (z + o) % NZ], dst_ref=brecv.at[core, slot],
            send_sem=aa_s.at[way], recv_sem=aa_r.at[core],
            device_id=((z + o) % NZ, home * 2 + side), device_id_type=MESH,
        )

    for o in FAR_FIRST:
        aa_copy(core, o).start()
        aa_copy(1 - core, o).start()
    aa_copy(1 - core, 0).start()

    @pl.when(home != chip)
    def _():
        aa_copy(core, 0).start()

    @pl.when(home == chip)
    def _():
        brecv[core, slot] = asend[core, z]

    wo_step(8)
    take(wog.at[1 - core], ws_r.at[0])
    take(brecv.at[1 - core], aa_r.at[1 - core])

    @pl.when((home != chip) | (gw.mine != z))
    def _():
        take(brecv.at[core], aa_r.at[core])

    @pl.when((home == chip) & (gw.mine == z))
    def _():
        take(brecv.at[core, pl.ds(0, NZ - 1)], aa_r.at[core])

    rows = [brecv[k].astype(F32).reshape(HALF, HD).astype(BF) for k in range(2)]
    rows = jnp.concatenate(rows, axis=1)

    def sum_copy(phase, half, p, o):
        along_x = (half == 0) == (phase == 0)
        to = at((x + o) % 4, y) if along_x else at(x, (y + o) % 4)
        slot = ((x if along_x else y) + o) % 4
        src, dst, ss, sr = ((ts, tr, t_s, t_r), (us, ur, u_s, u_r))[phase]
        return pltpu.make_async_remote_copy(
            src_ref=src.at[half, p, slot], dst_ref=dst.at[half, p, o],
            send_sem=ss.at[half, p], recv_sem=sr.at[half, p],
            device_id=to, device_id_type=MESH,
        )

    per = WIDE // BLK
    for p in range(PIECES):
        for half in range(2):
            for i in range(per):
                j = half * 8 + p * per + i
                cols = slice(i * BLK, (i + 1) * BLK)
                term = dot(rows, jnp.concatenate([wog[0, j], wog[1, j]], axis=0))
                term = term.reshape(4, 4, 8, BLK)
                for q in range(4):
                    mine = term[q] if half == 0 else term[:, q]
                    ts[half, p, q, :, cols] = mine.reshape(32, BLK).astype(BF)
            for o in (2, 1, 3):
                sum_copy(0, half, p, o).start()
    for p in range(PIECES):
        for half in range(2):
            total = ts[half, p, x if half == 0 else y].astype(F32)
            take(tr.at[half, p, pl.ds(1, 3)], t_r.at[half, p])
            for o in (1, 2, 3):
                total = total + tr[half, p, o].astype(F32)
            us[half, p] = total.reshape(4, 8, WIDE).astype(BF)
            for o in (2, 1, 3):
                sum_copy(1, half, p, o).start()

    take(xsend.at[pl.ds(0, NZ - 1)], xa_s.at[0])
    x_sib(core).wait_send()
    gw.drain()
    take(wall.at[pl.ds(0, 5)], rs_s.at[0])
    take(wall.at[pl.ds(0, 5)], rs_s.at[1])
    take(wall.at[pl.ds(0, 5)], wo_s.at[0])
    take(wog.at[core], ws_s.at[0])
    take(wall.at[pl.ds(0, 2)], qkv_s.at[0])
    take(nsend.at[pl.ds(1, 3)], nd_s.at[0])
    take(dsend.at[pl.ds(1, 3)], nd_s.at[1])
    take(asend.at[1 - core], aa_s.at[1])

    @pl.when(home != chip)
    def _():
        take(asend.at[core], aa_s.at[0])

    @pl.when(home == chip)
    def _():
        take(asend.at[core, pl.ds(0, NZ - 1)], aa_s.at[0])

    for p in range(PIECES):
        for half in range(2):
            take(ts.at[half, p, pl.ds(0, 3)], t_s.at[half, p])

    for p in range(PIECES):
        for half in range(2):
            total = us[half, p, y if half == 0 else x].astype(F32)
            take(ur.at[half, p, pl.ds(1, 3)], u_r.at[half, p])
            for o in (1, 2, 3):
                total = total + ur[half, p, o].astype(F32)
            first = half * 8 * BLK + p * WIDE
            out_ref[:, first:first + WIDE] = total.astype(BF)
    for p in range(PIECES):
        for half in range(2):
            take(us.at[half, p, pl.ds(0, 3)], u_s.at[half, p])


def body(latents, levels, order, level_table, q_gain, k_gain, w_qkv, w_out):
    vmem = pl.BlockSpec(memory_space=pltpu.VMEM)
    smem = pl.BlockSpec(memory_space=pltpu.SMEM)
    hbm = pl.BlockSpec(memory_space=pl.ANY)
    dma = pltpu.SemaphoreType.DMA
    return pl.pallas_call(
        kernel,
        out_shape=jax.ShapeDtypeStruct(latents.shape, BF),
        in_specs=[hbm, smem, smem, hbm, hbm, hbm, hbm, hbm],
        out_specs=vmem,
        scratch_shapes=[
            pltpu.VMEM(latents.shape, BF),
            pltpu.VMEM(level_table.shape, F32),
            pltpu.VMEM((1, HD), F32),
            pltpu.VMEM((1, HD), F32),
            pltpu.VMEM((16, BLK, BLK), BF),
            pltpu.VMEM((NZ, 8, BLK), BF),
            pltpu.VMEM((2, NZ, 8, BLK), BF),
            pltpu.VMEM((NT, BLK), BF),
            pltpu.VMEM((2, NT, BLK), F32),
            pltpu.VMEM((2, 8, NT, BLK), BF),
            pltpu.VMEM((2, 8, NT, BLK), BF),
            pltpu.VMEM((NT, NT), F32),
            pltpu.VMEM((4, NT, HD), BF),
            pltpu.VMEM((4, NT, HD), BF),
            pltpu.VMEM((4, HD, NT), BF),
            pltpu.VMEM((4, HD, NT), BF),
            pltpu.VMEM((4, HD, NT), BF),
            pltpu.VMEM((4, 8, NT), F32),
            pltpu.VMEM((4, 8, NT), F32),
            pltpu.VMEM((4, HD, NT), F32),
            pltpu.VMEM((4, 1, NT), F32),
            pltpu.VMEM((2, NZ, HD, BLK), BF),
            pltpu.VMEM((2, NZ, 8, HD), BF),
            pltpu.VMEM((2, NZ, 8, HD), BF),
            pltpu.VMEM((2, PIECES, 4, 32, WIDE), BF),
            pltpu.VMEM((2, PIECES, 4, 32, WIDE), BF),
            pltpu.VMEM((2, PIECES, 4, 8, WIDE), BF),
            pltpu.VMEM((2, PIECES, 4, 8, WIDE), BF),
            dma((6,)),
            dma((1,)), dma((1,)),
            dma((1,)), dma((1,)),
            dma((2, 2, 3)), dma((2, PARTS, 16)),
            dma((1,)), dma((2, 8)),
            dma((1,)), dma((1,)),
            dma((2,)), dma((2, 8, 2)),
            dma((1,)), dma((3, 4)),
            dma((2,)), dma((2, 4)),
            dma((2,)), dma((2,)),
            dma((2, PIECES)), dma((2, PIECES)),
            dma((2, PIECES)), dma((2, PIECES)),
        ],
        compiler_params=pltpu.CompilerParams(
            collective_id=0, has_side_effects=True, vmem_limit_bytes=60 * 2**20
        ),
        name="spans",
    )(
        latents, levels, order, level_table,
        q_gain.reshape(1, HD), k_gain.reshape(1, HD), w_qkv, w_out,
    )


def solution(mesh):
    placed = (
        P(("span", "seq"), None),
        P("span"),
        P(),
        P(),
        P(),
        P(),
        P("span", "seq"),
        P("seq", "span"),
    )
    return jax.shard_map(
        body, mesh=mesh, in_specs=placed, out_specs=P(("span", "seq"), None), check_vma=False
    )
```

```python
import jax
import jax.numpy as jnp
from jax import lax
from jax.experimental import pallas as pl
from jax.experimental.pallas import tpu as pltpu
from jax.sharding import PartitionSpec as P

HD = 128
NZ = 16
BF = jnp.bfloat16
F32 = jnp.float32
MESH = pl.DeviceIdType.MESH
BLK = 384
NT = 256
HALF = 128
FAR_FIRST = (8, 7, 9, 6, 10, 5, 11, 4, 12, 3, 13, 2, 14, 1, 15)
FIRST = 6
PARTS = 1
WO_AT = {0: 3, 7: 4}
PIECES = 2
WIDE = 8 * BLK // PIECES


def dot(a, b):
    return jnp.dot(a, b, preferred_element_type=F32)


def take(ref, sem):
    pltpu.make_async_copy(ref, ref, sem).wait()


class PlaneGather:
    def __init__(self, buf, rows, x, y, at, s1, rs):
        self.buf, self.rows, self.x, self.y, self.at = buf, rows, x, y, at
        self.s1, self.rs = s1, rs
        self.mine = ((x + 4 - y) % 4) * 4 + y

    @staticmethod
    def place(block):
        return block % 4, (block + block // 4) % 4

    def part(self, block, half, part):
        rows = self.rows // PARTS
        return self.buf.at[block, pl.ds(half * self.rows + part * rows, rows)]

    def target(self, half, phase, o):
        along_x = (half == 0) == (phase == 1)
        if along_x:
            return self.at((self.x + o) % 4, self.y)
        return self.at(self.x, (self.y + o) % 4)

    def copy(self, block, half, part, phase, i):
        o = (1, 3, 2)[i]
        sem = self.s1.at[phase - 1, half, i]
        ref = self.part(block, half, part)
        return pltpu.make_async_remote_copy(
            src_ref=ref,
            dst_ref=ref,
            send_sem=sem,
            recv_sem=self.rs.at[half, part, block],
            device_id=self.target(half, phase, o),
            device_id_type=MESH,
        )

    def first(self):
        for part in range(PARTS):
            for i in range(3):
                for half in range(2):
                    self.copy(self.mine, half, part, 1, i).start()

    def wait_block(self, block, half, part):
        self.copy(block, half, part, 1, 0).wait_recv()

    def second(self, block, part):
        by, bx = self.place(block)
        for half in range(2):
            same = (by == self.y) if half == 0 else (bx == self.x)

            @pl.when(same)
            def _(half=half):
                @pl.when(block != self.mine)
                def _():
                    self.wait_block(block, half, part)

                for i in range(3):
                    self.copy(block, half, part, 2, i).start()

    def use(self, block):
        by, bx = self.place(block)

        @pl.when(by != self.y)
        def _():
            for part in range(PARTS):
                self.wait_block(block, 0, part)

        @pl.when(bx != self.x)
        def _():
            for part in range(PARTS):
                self.wait_block(block, 1, part)

    def drain(self):
        for half in range(2):
            for i in range(3):
                self.copy(self.mine, half, 0, 1, i).wait_send()
                take(self.buf.at[pl.ds(0, 2)], self.s1.at[1, half, i])


def kernel(
    lat_hbm, lev_ref, ord_ref, tab_hbm, qg_hbm, kg_hbm, w_ref, wo_ref, out_ref,
    lat_ref, tab_ref, qg_ref, kg_ref, wall, xsend, xr, xin, part, cws, cwr, mask,
    qs, ks, vs, nsend, nrecv, dsend, drecv, tops, lows, wog, asend, brecv, ts, tr, us, ur,
    load_sem, xa_s, xa_r, sib_s, sib_r, w1, wr, wo_s, wo_r, ws_s, ws_r,
    rs_s, rs_r, qkv_s, qkv_r, nd_s, nd_r, aa_s, aa_r, t_s, t_r, u_s, u_r,
):
    z = lax.axis_index("span")
    s = lax.axis_index("seq")
    core = s % 2
    chip = s // 2
    x = chip % 4
    y = chip // 4

    def at(px, py):
        return (z, (py * 4 + px) * 2 + core)

    def along_z(o):
        return ((z + o) % NZ, s)

    sibling = (z, chip * 2 + 1 - core)

    gw = PlaneGather(wall, BLK // 2, x, y, at, w1, wr)
    loads = [
        pltpu.make_async_copy(src, dst, load_sem.at[i])
        for i, (src, dst) in enumerate((
            (lat_hbm, lat_ref), (tab_hbm, tab_ref), (w_ref, wall.at[gw.mine]),
            (wo_ref, wog.at[core, z]), (qg_hbm, qg_ref), (kg_hbm, kg_ref),
        ))
    ]
    for load in loads:
        load.start()

    barrier = pltpu.get_barrier_semaphore()
    for o in FAR_FIRST:
        pl.semaphore_signal(barrier, inc=1, device_id=along_z(o), device_id_type=MESH)
    for o in (2, 1, 3):
        pl.semaphore_signal(barrier, inc=1, device_id=at((x + o) % 4, y), device_id_type=MESH)
        pl.semaphore_signal(barrier, inc=1, device_id=at(x, (y + o) % 4), device_id_type=MESH)
    pl.semaphore_signal(barrier, inc=1, device_id=sibling, device_id_type=MESH)

    for load in loads:
        load.wait()
    width = lat_ref.shape[1]
    level = lev_ref[0]
    row = tab_ref[pl.ds(level, 1), :]
    values = lat_ref[...].astype(F32)
    center = values - jnp.mean(values, axis=1, keepdims=True)
    spread = jnp.mean(center * center, axis=1, keepdims=True)
    modulated = center * lax.rsqrt(spread + 1e-06) * (1.0 + row[:, width:]) + row[:, :width]
    modulated = modulated.astype(BF)
    for j in range(NZ):
        xsend[j] = modulated[:, j * BLK:(j + 1) * BLK]
    xr[core, z] = xsend[z]

    def wo_copy(way, t, arrival=False):
        back = t + (1 if arrival else 0)
        slot = (z + NZ - back) % NZ if way == 0 else (z + back) % NZ
        ref = wog.at[core, slot]
        if t == 7:
            ref = wog.at[core, slot, pl.ds(way * (HD // 2), HD // 2)]
        return pltpu.make_async_remote_copy(
            src_ref=ref, dst_ref=ref,
            send_sem=wo_s.at[0], recv_sem=wo_r.at[way, t],
            device_id=along_z(1 if way == 0 else NZ - 1), device_id_type=MESH,
        )

    def wo_sib(side, o):
        ref = wog.at[side, (z + o) % NZ]
        return pltpu.make_async_remote_copy(
            src_ref=ref, dst_ref=ref, send_sem=ws_s.at[0], recv_sem=ws_r.at[0],
            device_id=sibling, device_id_type=MESH,
        )

    def wo_step(t):
        if t > 0:
            for way in range(2):
                wo_copy(way, t - 1, True).wait_recv()
        if t < 8:
            for way in range(2):
                wo_copy(way, t).start()
        if t == 0 or t == 8:
            wo_sib(core, t).start()
        else:
            wo_sib(core, t).start()
            wo_sib(core, NZ - t).start()

    def x_copy(o):
        return pltpu.make_async_remote_copy(
            src_ref=xsend.at[(z + o) % NZ], dst_ref=xr.at[core, z],
            send_sem=xa_s.at[0], recv_sem=xa_r.at[0],
            device_id=along_z(o), device_id_type=MESH,
        )

    pl.semaphore_wait(barrier, 22)
    gw.first()

    for o in FAR_FIRST:
        x_copy(o).start()
    wo_step(0)

    key_span = (lax.broadcasted_iota(jnp.int32, (NT, HD), 0) % HALF) // 8
    query_span = (lax.broadcasted_iota(jnp.int32, (8, NT), 1) % HALF) // 8
    key_order = jnp.zeros((NT, HD), jnp.int32)
    query_order = jnp.zeros((8, NT), jnp.int32)
    for j in range(NZ):
        place = ord_ref[j]
        key_order = jnp.where(key_span == j, place, key_order)
        query_order = jnp.where(query_span == j, place, query_order)
    key_order = jnp.concatenate([key_order, key_order], axis=1)
    mask[...] = jnp.where(key_order <= query_order[0:1, :], 1.0, 0.0)

    take(xr.at[core, pl.ds(0, NZ - 1)], xa_r.at[0])

    def x_sib(slot):
        return pltpu.make_async_remote_copy(
            src_ref=xr.at[slot], dst_ref=xr.at[slot],
            send_sem=sib_s.at[0], recv_sem=sib_r.at[0],
            device_id=sibling, device_id_type=MESH,
        )

    x_sib(core).start()

    def place_of(t, way):
        return (z + 8 - t) % NZ if way == 0 else (z + 8 + t) % NZ

    order_of_use = [place_of(0, 0)]
    for t in range(1, 8):
        order_of_use += [place_of(t, 0), place_of(t, 1)]
    order_of_use.append(z)
    for piece in range(PARTS):
        for block in order_of_use[:FIRST]:
            gw.second(block, piece)

    wo_step(1)
    x_sib(1 - core).wait_recv()
    xin[...] = xr[...].astype(F32).reshape(NT, BLK).astype(BF)

    wo_step(2)

    def rs_copy(way, t, p):
        rows = pl.ds(p * HALF, HALF)
        return pltpu.make_async_remote_copy(
            src_ref=cws.at[way, t, rows], dst_ref=cwr.at[way, t, rows],
            send_sem=rs_s.at[way], recv_sem=rs_r.at[way, t, p],
            device_id=along_z(1 if way == 0 else NZ - 1), device_id_type=MESH,
        )

    for t in range(8):
        if t == 0:
            block = place_of(0, 0)
            gw.use(block)
            cws[0, 0, 0:HALF] = dot(xin[0:HALF], wall[block]).astype(BF)
            rs_copy(0, 0, 0).start()
            cws[1, 0, HALF:NT] = dot(xin[HALF:NT], wall[block]).astype(BF)
            rs_copy(1, 0, 1).start()
        else:
            for way in range(2):
                block = place_of(t, way)
                gw.use(block)
                part[way] = dot(xin[...], wall[block])
            for p in range(2):
                rows = slice(p * HALF, (p + 1) * HALF)
                for way in range(2):
                    total = part[way, rows]
                    if t > 1 or p == way:
                        rs_copy(way, t - 1, p).wait_recv()
                        total = total + cwr[way, t - 1, rows].astype(F32)
                    cws[way, t, rows] = total.astype(BF)
                    rs_copy(way, t, p).start()
        for block in order_of_use[FIRST + 2 * t:FIRST + 2 * t + 2]:
            for piece in range(PARTS):
                gw.second(block, piece)
        if t in WO_AT:
            wo_step(WO_AT[t])
    gw.use(z)
    part[0] = dot(xin[...], wall[z])

    def head_norm(block, gain):
        square = jnp.mean(block * block, axis=-1, keepdims=True)
        return (block * lax.rsqrt(square + 1e-06) * gain).astype(BF)

    def qkv_copy(which, o, p, me):
        ref = (ks, vs, qs)[which].at[me]
        half = pl.ds(p * HALF, HALF)
        ref = ref.at[:, half] if which == 1 else ref.at[half]
        to = at(x, (y + o) % 4) if which < 2 else at((x + o) % 4, y)
        return pltpu.make_async_remote_copy(
            src_ref=ref, dst_ref=ref,
            send_sem=qkv_s.at[0], recv_sem=qkv_r.at[which, o],
            device_id=to, device_id_type=MESH,
        )

    for p in range(2):
        rows = slice(p * HALF, (p + 1) * HALF)
        for way in range(2):
            rs_copy(way, 7, p).wait_recv()
        total = part[0, rows] + cwr[0, 7, rows].astype(F32) + cwr[1, 7, rows].astype(F32)
        total = total.astype(BF).astype(F32)
        ks[y, rows] = head_norm(total[:, HD:2 * HD], kg_ref[...])
        vs[y, :, rows] = jnp.transpose(total[:, 2 * HD:3 * HD]).astype(BF)
        for o in (2, 1, 3):
            for which in range(2):
                qkv_copy(which, o, p, y).start()
        qs[x, rows] = head_norm(total[:, 0:HD], qg_ref[...])
        for o in (2, 1, 3):
            qkv_copy(2, o, p, x).start()
    wo_step(5)
    def nd_copy(which, o):
        src, dst = ((nsend, nrecv), (dsend, drecv))[which]
        return pltpu.make_async_remote_copy(
            src_ref=src.at[o], dst_ref=dst.at[o],
            send_sem=nd_s.at[which], recv_sem=nd_r.at[which, o],
            device_id=at((x + o) % 4, y), device_id_type=MESH,
        )

    def attend(first, j, o):
        queries = qs[(x + o) % 4]
        scores = lax.dot_general(
            ks[j], queries, (((1,), (1,)), ((), ())), preferred_element_type=F32
        ) * HD ** (-0.5)
        probs = jnp.exp(scores) * mask[...]
        low = jnp.sum(probs, axis=0, keepdims=True)
        top = dot(vs[j], probs.astype(BF))
        if not first:
            low = low + lows[o]
            top = top + tops[o]
        return top, low

    def attend_all(first, j):
        for o in range(4):
            tops[o], lows[o] = attend(first, j, o)

    tops[0], lows[0] = attend(True, y, 0)
    for o in (1, 3, 2):
        take(qs.at[(x + 4 - o) % 4], qkv_r.at[2, o])
        tops[4 - o], lows[4 - o] = attend(True, y, 4 - o)
    for o in (1, 3):
        take(ks.at[(y + 4 - o) % 4], qkv_r.at[0, o])
        take(vs.at[(y + 4 - o) % 4], qkv_r.at[1, o])
        attend_all(False, (y + 4 - o) % 4)
        if o == 1:
            wo_step(6)
    take(ks.at[(y + 2) % 4], qkv_r.at[0, 2])
    take(vs.at[(y + 2) % 4], qkv_r.at[1, 2])
    for o in (2, 1, 3):
        top, low = attend(False, (y + 2) % 4, o)
        nsend[o] = top.astype(BF)
        dsend[o] = jnp.broadcast_to(low, (8, NT))
        nd_copy(0, o).start()
        nd_copy(1, o).start()
    top, low = attend(False, (y + 2) % 4, 0)
    wo_step(7)
    for o in (2, 1, 3):
        nd_copy(0, o).wait_recv()
        nd_copy(1, o).wait_recv()
        top = top + nrecv[o].astype(F32)
        low = low + drecv[o][0:1, :]
    asend[...] = jnp.transpose(top / low).reshape(2, NZ, 8, HD).astype(BF)

    home_y, home_x = gw.place(z)
    home = home_y * 4 + home_x
    slot = x * 4 + y

    def aa_copy(side, o):
        way = 0 if side is core else 1
        return pltpu.make_async_remote_copy(
            src_ref=asend.at[side, (z + o) % NZ], dst_ref=brecv.at[core, slot],
            send_sem=aa_s.at[way], recv_sem=aa_r.at[core],
            device_id=((z + o) % NZ, home * 2 + side), device_id_type=MESH,
        )

    for o in FAR_FIRST:
        aa_copy(core, o).start()
        aa_copy(1 - core, o).start()
    aa_copy(1 - core, 0).start()

    @pl.when(home != chip)
    def _():
        aa_copy(core, 0).start()

    @pl.when(home == chip)
    def _():
        brecv[core, slot] = asend[core, z]

    wo_step(8)
    take(wog.at[1 - core], ws_r.at[0])
    take(brecv.at[1 - core], aa_r.at[1 - core])

    @pl.when((home != chip) | (gw.mine != z))
    def _():
        take(brecv.at[core], aa_r.at[core])

    @pl.when((home == chip) & (gw.mine == z))
    def _():
        take(brecv.at[core, pl.ds(0, NZ - 1)], aa_r.at[core])

    rows = [brecv[k].astype(F32).reshape(HALF, HD).astype(BF) for k in range(2)]
    rows = jnp.concatenate(rows, axis=1)

    def sum_copy(phase, half, p, o):
        along_x = (half == 0) == (phase == 0)
        to = at((x + o) % 4, y) if along_x else at(x, (y + o) % 4)
        slot = ((x if along_x else y) + o) % 4
        src, dst, ss, sr = ((ts, tr, t_s, t_r), (us, ur, u_s, u_r))[phase]
        return pltpu.make_async_remote_copy(
            src_ref=src.at[half, p, slot], dst_ref=dst.at[half, p, o],
            send_sem=ss.at[half, p], recv_sem=sr.at[half, p],
            device_id=to, device_id_type=MESH,
        )

    per = WIDE // BLK
    for p in range(PIECES):
        for half in range(2):
            for i in range(per):
                j = half * 8 + p * per + i
                cols = slice(i * BLK, (i + 1) * BLK)
                term = dot(rows, jnp.concatenate([wog[0, j], wog[1, j]], axis=0))
                term = term.reshape(4, 4, 8, BLK)
                for q in range(4):
                    mine = term[q] if half == 0 else term[:, q]
                    ts[half, p, q, :, cols] = mine.reshape(32, BLK).astype(BF)
            for o in (2, 1, 3):
                sum_copy(0, half, p, o).start()
    for p in range(PIECES):
        for half in range(2):
            total = ts[half, p, x if half == 0 else y].astype(F32)
            take(tr.at[half, p, pl.ds(1, 3)], t_r.at[half, p])
            for o in (1, 2, 3):
                total = total + tr[half, p, o].astype(F32)
            us[half, p] = total.reshape(4, 8, WIDE).astype(BF)
            for o in (2, 1, 3):
                sum_copy(1, half, p, o).start()

    take(xsend.at[pl.ds(0, NZ - 1)], xa_s.at[0])
    x_sib(core).wait_send()
    gw.drain()
    take(wall.at[pl.ds(0, 5)], rs_s.at[0])
    take(wall.at[pl.ds(0, 5)], rs_s.at[1])
    take(wall.at[pl.ds(0, 5)], wo_s.at[0])
    take(wog.at[core], ws_s.at[0])
    take(wall.at[pl.ds(0, 2)], qkv_s.at[0])
    take(nsend.at[pl.ds(1, 3)], nd_s.at[0])
    take(dsend.at[pl.ds(1, 3)], nd_s.at[1])
    take(asend.at[1 - core], aa_s.at[1])

    @pl.when(home != chip)
    def _():
        take(asend.at[core], aa_s.at[0])

    @pl.when(home == chip)
    def _():
        take(asend.at[core, pl.ds(0, NZ - 1)], aa_s.at[0])

    for p in range(PIECES):
        for half in range(2):
            take(ts.at[half, p, pl.ds(0, 3)], t_s.at[half, p])

    for p in range(PIECES):
        for half in range(2):
            total = us[half, p, y if half == 0 else x].astype(F32)
            take(ur.at[half, p, pl.ds(1, 3)], u_r.at[half, p])
            for o in (1, 2, 3):
                total = total + ur[half, p, o].astype(F32)
            first = half * 8 * BLK + p * WIDE
            out_ref[:, first:first + WIDE] = total.astype(BF)
    for p in range(PIECES):
        for half in range(2):
            take(us.at[half, p, pl.ds(0, 3)], u_s.at[half, p])


def body(latents, levels, order, level_table, q_gain, k_gain, w_qkv, w_out):
    vmem = pl.BlockSpec(memory_space=pltpu.VMEM)
    smem = pl.BlockSpec(memory_space=pltpu.SMEM)
    hbm = pl.BlockSpec(memory_space=pl.ANY)
    dma = pltpu.SemaphoreType.DMA
    return pl.pallas_call(
        kernel,
        out_shape=jax.ShapeDtypeStruct(latents.shape, BF),
        in_specs=[hbm, smem, smem, hbm, hbm, hbm, hbm, hbm],
        out_specs=vmem,
        scratch_shapes=[
            pltpu.VMEM(latents.shape, BF),
            pltpu.VMEM(level_table.shape, F32),
            pltpu.VMEM((1, HD), F32),
            pltpu.VMEM((1, HD), F32),
            pltpu.VMEM((16, BLK, BLK), BF),
            pltpu.VMEM((NZ, 8, BLK), BF),
            pltpu.VMEM((2, NZ, 8, BLK), BF),
            pltpu.VMEM((NT, BLK), BF),
            pltpu.VMEM((2, NT, BLK), F32),
            pltpu.VMEM((2, 8, NT, BLK), BF),
            pltpu.VMEM((2, 8, NT, BLK), BF),
            pltpu.VMEM((NT, NT), F32),
            pltpu.VMEM((4, NT, HD), BF),
            pltpu.VMEM((4, NT, HD), BF),
            pltpu.VMEM((4, HD, NT), BF),
            pltpu.VMEM((4, HD, NT), BF),
            pltpu.VMEM((4, HD, NT), BF),
            pltpu.VMEM((4, 8, NT), F32),
            pltpu.VMEM((4, 8, NT), F32),
            pltpu.VMEM((4, HD, NT), F32),
            pltpu.VMEM((4, 1, NT), F32),
            pltpu.VMEM((2, NZ, HD, BLK), BF),
            pltpu.VMEM((2, NZ, 8, HD), BF),
            pltpu.VMEM((2, NZ, 8, HD), BF),
            pltpu.VMEM((2, PIECES, 4, 32, WIDE), BF),
            pltpu.VMEM((2, PIECES, 4, 32, WIDE), BF),
            pltpu.VMEM((2, PIECES, 4, 8, WIDE), BF),
            pltpu.VMEM((2, PIECES, 4, 8, WIDE), BF),
            dma((6,)),
            dma((1,)), dma((1,)),
            dma((1,)), dma((1,)),
            dma((2, 2, 3)), dma((2, PARTS, 16)),
            dma((1,)), dma((2, 8)),
            dma((1,)), dma((1,)),
            dma((2,)), dma((2, 8, 2)),
            dma((1,)), dma((3, 4)),
            dma((2,)), dma((2, 4)),
            dma((2,)), dma((2,)),
            dma((2, PIECES)), dma((2, PIECES)),
            dma((2, PIECES)), dma((2, PIECES)),
        ],
        compiler_params=pltpu.CompilerParams(
            collective_id=0, has_side_effects=True, vmem_limit_bytes=60 * 2**20
        ),
        name="spans",
    )(
        latents, levels, order, level_table,
        q_gain.reshape(1, HD), k_gain.reshape(1, HD), w_qkv, w_out,
    )


def solution(mesh):
    placed = (
        P(("span", "seq"), None),
        P("span"),
        P(),
        P(),
        P(),
        P(),
        P("span", "seq"),
        P("seq", "span"),
    )
    return jax.shard_map(
        body, mesh=mesh, in_specs=placed, out_specs=P(("span", "seq"), None), check_vma=False
    )
```
